128 devices in a mesh: row: 8 (over y, z_lo), col: 16 (over z_hi, x, core).
Axes of the slice: x: 4, y: 4, z: 4 (z_hi: 2, z_lo: 2; z = z_hi * 2 + z_lo), core: 2. Of those that a mesh axis runs over, the one named last changes fastest.
Arguments:
- velocity: float32 [3, 4, 512, 2048], P(None, None, 'row', 'col'), may hold values from -6 to 6
- stress: float32 [6, 4, 512, 2048], P(None, None, 'row', 'col'), may hold values from -6 to 6
- buoyancy: float32 [4, 512, 2048], P(None, 'row', 'col'), may hold values from 0.2 to 0.4
- lame: float32 [4, 512, 2048], P(None, 'row', 'col'), may hold values from 0.08 to 0.2
- shear: float32 [4, 512, 2048], P(None, 'row', 'col'), may hold values from 0.08 to 0.2
- kernel: bfloat16 [12, 3, 2, 2048, 512], P(None, None, None, ('row', 'col')), may hold values from -1.1953125 to 1.1953125
- history: bfloat16 [11, 3, 2, 2048, 512], P(None, None, None, ('row', 'col')), may hold values from -6 to 6
Outputs:
- new_velocity: float32 [3, 4, 512, 2048], P(None, None, 'row', 'col')
- new_stress: float32 [6, 4, 512, 2048], P(None, None, 'row', 'col')
- spectra: float32 [2, 3, 2, 2048, 512], P(None, None, None, ('row', 'col'))
The draws below stay inside these ranges and needn't reach their ends.
All inputs are finite; a program needn't handle non-finite values.
Results may differ from the reference program's by a relative error of at most 0.0003.
Values sent between devices are 32-bit elements; how exact they have to be, the bound alone decides.
A program may use at most 128 MiB of HBM per device.

```python
import math
import jax
import jax.numpy as jnp

LAYERS = 4
HIST = 12
STEPS = 2
NX = 512
NY = 2048


def shard_levels(stream_key, extent, split, least, high):
    factor_of, own = 1.0, jax.random.fold_in(stream_key, 6)
    for axis_at, blocks in split:
        heights = jnp.exp(jax.random.uniform(jax.random.fold_in(own, axis_at), (blocks,), jnp.float32, least / len(split), high / len(split)))
        factor_of = factor_of * jnp.repeat(heights, extent[axis_at] // blocks).reshape([-1 if axis == axis_at else 1 for axis in range(len(extent))])
    return factor_of


def centred(own_key, dims, deviation, bound, cuts=(), dtype=jnp.bfloat16):
    values = deviation * jax.random.normal(own_key, dims, jnp.float32)
    if cuts:
        values = values * shard_levels(own_key, dims, cuts, -0.22, 0.18)
    return jnp.clip(values, -bound, bound).astype(dtype)


def setup_inputs(seed: int = 0) -> dict:
    splits = jax.random.split(jax.random.key(seed), 8)
    velocity = centred(splits[0], (3, LAYERS, NX, NY), 1.0, 6.0, ((2, 8), (3, 16)), jnp.float32)
    stress = centred(splits[1], (6, LAYERS, NX, NY), 1.0, 6.0, ((2, 8), (3, 16)), jnp.float32)
    buoyancy = jnp.clip(jnp.exp(math.log(0.4) - 0.6931472 * jax.random.uniform(splits[2], (LAYERS, NX, NY), jnp.float32) ** shard_levels(splits[2], (LAYERS, NX, NY), ((1, 8), (2, 16)), -0.2, 0.2)), 0.2, 0.4)
    lame = jnp.clip(jnp.exp(math.log(0.2) - 0.91629077 * jax.random.uniform(splits[3], (LAYERS, NX, NY), jnp.float32) ** shard_levels(splits[3], (LAYERS, NX, NY), ((1, 8), (2, 16)), -0.2, 0.2)), 0.08, 0.2)
    shear = jnp.clip(jnp.exp(math.log(0.2) - 0.91629077 * jax.random.uniform(splits[4], (LAYERS, NX, NY), jnp.float32) ** shard_levels(splits[4], (LAYERS, NX, NY), ((1, 8), (2, 16)), -0.2, 0.2)), 0.08, 0.2)
    kernel = centred(splits[5], (HIST, 3, 2, NY, NX), 0.2, 1.1953125, ((3, 128),))
    history = centred(splits[6], (HIST - 1, 3, 2, NY, NX), 1.0, 6.0, ((3, 128),))
    return dict(velocity=velocity, stress=stress, buoyancy=buoyancy, lame=lame, shear=shear, kernel=kernel, history=history)


near_weight = 2.0 / 3.0
far_weight = -1.0 / 12.0


def plane_deriv(values, along_dim):
    return near_weight * (jnp.roll(values, -1, along_dim) - jnp.roll(values, 1, along_dim)) + far_weight * (jnp.roll(values, -2, along_dim) - jnp.roll(values, 2, along_dim))


def depth_deriv(values):
    layers = values.shape[1]
    padded = jnp.pad(values, ((0, 0), (2, 2), (0, 0), (0, 0)))
    return near_weight * (padded[:, 3:layers + 3] - padded[:, 1:layers + 1]) + far_weight * (padded[:, 4:layers + 4] - padded[:, 0:layers])


def complex_entry(source, index):
    return source[index, :, 0].astype(jnp.float32) + 1j * source[index, :, 1].astype(jnp.float32)


def update_stress(stress, grad_x, grad_y, grad_z, lame, shear, traction):
    diverge = grad_x[0] + grad_y[1] + grad_z[2]
    result = jnp.stack((
        stress[0] + lame * diverge + 2.0 * shear * grad_x[0],
        stress[1] + lame * diverge + 2.0 * shear * grad_y[1],
        stress[2] + lame * diverge + 2.0 * shear * grad_z[2],
        stress[3] + shear * (grad_y[0] + grad_x[1]),
        stress[4] + shear * (grad_z[0] + grad_x[2]),
        stress[5] + shear * (grad_z[1] + grad_y[2])))
    result = result.at[2, 0].add(traction[2])
    result = result.at[4, 0].add(traction[0])
    return result.at[5, 0].add(traction[1])


def reference(velocity, stress, buoyancy, lame, shear, kernel, history):
    earlier = []
    for step_index in range(STEPS):
        along_x = plane_deriv(jnp.stack((stress[0], stress[3], stress[4])), 2)
        along_y = plane_deriv(jnp.stack((stress[3], stress[1], stress[5])), 3)
        along_z = depth_deriv(jnp.stack((stress[4], stress[5], stress[2])))
        velocity = velocity + buoyancy * (along_x + along_y + along_z)
        spectrum = jnp.transpose(jnp.fft.fft2(velocity[:, 0], norm="ortho"), (0, 2, 1))
        total = complex_entry(kernel, 0) * spectrum
        for lag in range(1, HIST):
            if lag - 1 < len(earlier):
                source = earlier[lag - 1]
            else:
                source = complex_entry(history, lag - 1 - len(earlier))
            total = total + complex_entry(kernel, lag) * source
        traction = jnp.real(jnp.fft.ifft2(jnp.transpose(total, (0, 2, 1)), norm="ortho"))
        grad_x = plane_deriv(velocity, 2)
        grad_y = plane_deriv(velocity, 3)
        grad_z = depth_deriv(velocity)
        stress = update_stress(stress, grad_x, grad_y, grad_z, lame, shear, traction)
        earlier = [spectrum] + earlier
    spectra = jnp.stack([jnp.stack((jnp.real(entry), jnp.imag(entry)), axis=1) for entry in reversed(earlier)])
    return velocity, stress, spectra
```

```python
import math

import jax
import jax.numpy as jnp
import numpy as np
from jax import lax
from jax.experimental import pallas as pl
from jax.experimental.pallas import tpu as pltpu
from jax.sharding import PartitionSpec as P

MESH = pl.DeviceIdType.MESH
F32, BF16 = jnp.float32, jnp.bfloat16
ROWS, COLS, DEVS = 8, 16, 128
NEAR, FAR = 2.0 / 3.0, -1.0 / 12.0
PLACE = (0, 3, 4, 1, 5, 2)
XX, XY, XZ, YY, YZ, ZZ = range(6)


def tables():
    def halves(a):
        hi = a.astype(BF16)
        lo = (a - hi.astype(np.float64)).astype(BF16)
        return hi, lo

    i128 = np.arange(128)
    ang = 2 * np.pi * (np.outer(i128, i128) % 128) / 128
    cos, sin = np.cos(ang), np.sin(ang)
    hi, lo = halves(np.concatenate([cos, sin], axis=1))
    left = np.concatenate([hi, hi, lo], axis=1)
    right = np.concatenate([hi, hi, lo], axis=0)
    j, c = np.arange(16), np.arange(16)
    ang = 2 * np.pi * (np.outer(j, c) % 16) / 16
    one = np.zeros((2, 4, 16, 16, 4))
    for xl in range(4):
        one[0, xl, :, :, xl] = np.cos(ang)
        one[1, xl, :, :, xl] = -np.sin(ang)
    one = one.reshape(128, 64) / 1024.0
    hi, lo = halves(one)
    first = np.concatenate([hi, hi, lo, lo], axis=1)
    hi, lo = halves(one.T)
    last = np.concatenate([hi, hi, lo], axis=1)
    small = np.zeros((48, 128), np.float32)
    ang = 2 * np.pi * np.outer(j, i128) / 2048
    small[0:16], small[16:32] = np.cos(ang), np.sin(ang)
    ang = 2 * np.pi * np.outer(np.arange(4), i128) / 512
    small[32:36], small[36:40] = np.cos(ang), np.sin(ang)
    th = 2 * np.pi * np.arange(512) / 512
    small[40:44] = (4 / 3 * np.sin(th) - 1 / 6 * np.sin(2 * th)).reshape(4, 128)
    th = 2 * np.pi * np.arange(2048) / 2048
    along = (4 / 3 * np.sin(th) - 1 / 6 * np.sin(2 * th)).reshape(128, 16, 1)
    along = np.broadcast_to(along, (128, 16, 128)).astype(np.float32)
    return left, right, first, last, small, along


def halves(x):
    hi = x.astype(BF16)
    return hi, (x - hi.astype(F32)).astype(BF16)


def dot(a, b, contract=((1,), (0,))):
    return lax.dot_general(a, b, (contract, ((), ())), preferred_element_type=F32)


def kernel_body(
    vel_in, str_in, buo_in, lam_in, she_in, ker_in, his_in,
    left_in, right_in, first_in, last_in, small_in, along_in,
    vel_out, str_out, spe_out,
    vpad, spad, coef, ker, his, left, right, first, last, small, along,
    pack, pack_low, pack_high, rows_in, buo_rows, send_a, recv_a, send_b, recv_b,
    rows_out, trac, part, spec,
    in_sem, out_sem, halo_send, halo_recv, col_send, col_recv, all_send, all_recv, own_sem,
):
    r, c = lax.axis_index("row"), lax.axis_index("col")
    me = r * COLS + c

    loads = []

    def load(src, dst):
        copy = pltpu.make_async_copy(src, dst, in_sem.at[len(loads)])
        copy.start()
        loads.append(copy)
        return copy

    stress_loads = [
        load(str_in.at[PLACE[k]], spad.at[k, :, pl.ds(8, 64), :]) for k in range(6)
    ]
    coef_loads = [load(buo_in, coef.at[0])]
    vel_load = load(vel_in, vpad.at[:, :, pl.ds(8, 64), :])
    conv_loads = [load(ker_in, ker), load(his_in, his)]
    table_loads = [
        load(left_in, left), load(right_in, right), load(first_in, first),
        load(last_in, last), load(small_in, small), load(along_in.at[me], along),
    ]
    coef_late = [load(lam_in, coef.at[1]), load(she_in, coef.at[2])]

    def device(k):
        t = lax.rem(me + k, DEVS)
        return (t // COLS, lax.rem(t, COLS))

    barrier = pltpu.get_barrier_semaphore()

    def greet(k, _):
        pl.semaphore_signal(barrier, inc=1, device_id=device(k), device_id_type=MESH)
        return 0

    lax.fori_loop(1, DEVS, greet, 0)

    up, down = (lax.rem(r + 1, ROWS), c), (lax.rem(r + ROWS - 1, ROWS), c)
    after, before = (r, lax.rem(c + 1, COLS)), (r, lax.rem(c + COLS - 1, COLS))

    lane = lax.broadcasted_iota(jnp.int32, (64, 128), 1)
    edge = jnp.logical_or(lane < 2, lane >= 126)

    def start_halo(n, pad, count, arrays):
        packed = jnp.zeros((64, 128), F32)
        for k, (comp, layer) in enumerate(arrays):
            f = pad[comp, layer, pl.ds(8, 64), :]
            packed += pltpu.roll(jnp.where(edge, f, 0.0), 4 * k + 2, 1)
        pack[n] = packed

        def remote(i, src, dst, to):
            copy = pltpu.make_async_remote_copy(
                src_ref=src, dst_ref=dst, send_sem=halo_send.at[n, i],
                recv_sem=halo_recv.at[n, i], device_id=to, device_id_type=MESH,
            )
            return copy

        copies = [
            remote(0, pad.at[pl.ds(0, count), :, pl.ds(64, 8), :],
                   pad.at[pl.ds(0, count), :, pl.ds(0, 8), :], up),
            remote(1, pad.at[pl.ds(0, count), :, pl.ds(8, 8), :],
                   pad.at[pl.ds(0, count), :, pl.ds(72, 8), :], down),
            remote(2, pack.at[n], pack_low.at[n], after),
            remote(3, pack.at[n], pack_high.at[n], before),
        ]
        return copies

    def edges_of(n):
        return jnp.where(lax.rem(lane, 4) >= 2, pack_high[n], pack_low[n])

    def dx(pad, comp, layer):
        def at(o):
            return pad[comp, layer, pl.ds(8 + o, 64), :]

        return NEAR * (at(1) - at(-1)) + FAR * (at(2) - at(-2))

    def dy(f, both, k):
        e = pltpu.roll(both, 128 - (4 * k + 2), 1)
        p1 = pltpu.roll(jnp.where(lane == 0, e, f), 127, 1)
        p2 = pltpu.roll(jnp.where(lane < 2, e, f), 126, 1)
        m1 = pltpu.roll(jnp.where(lane == 127, e, f), 1, 1)
        m2 = pltpu.roll(jnp.where(lane >= 126, e, f), 2, 1)
        return NEAR * (p1 - m1) + FAR * (p2 - m2)

    def dz(pad, comp, layer):
        total = None
        for o, w in ((1, NEAR), (-1, -NEAR), (2, FAR), (-2, -FAR)):
            if 0 <= layer + o < 4:
                term = w * pad[comp, layer + o, pl.ds(8, 64), :]
                total = term if total is None else total + term
        return total

    stress_y = [(k, l) for k in (XY, YY, YZ) for l in range(4)]
    vel_y = [(k, l) for k in range(3) for l in range(4)]

    def new_velocity(both, layer):
        along_x = [dx(spad, k, layer) for k in (XX, XY, XZ)]
        along_y = [
            dy(spad[k, layer, pl.ds(8, 64), :], both, 4 * i + layer)
            for i, k in enumerate((XY, YY, YZ))
        ]
        along_z = [dz(spad, k, layer) for k in (XZ, YZ, ZZ)]
        b = coef[0, layer]
        for i in range(3):
            vpad[i, layer, pl.ds(8, 64), :] = vpad[i, layer, pl.ds(8, 64), :] + b * (
                along_x[i] + along_y[i] + along_z[i]
            )

    def new_stress(both, layer):
        gx = [dx(vpad, i, layer) for i in range(3)]
        gy = [dy(vpad[i, layer, pl.ds(8, 64), :], both, 4 * i + layer) for i in range(3)]
        gz = [dz(vpad, i, layer) for i in range(3)]
        lam, she = coef[1, layer], coef[2, layer]
        spread = lam * (gx[0] + gy[1] + gz[2])
        adds = {
            XX: spread + 2.0 * she * gx[0], YY: spread + 2.0 * she * gy[1],
            ZZ: spread + 2.0 * she * gz[2], XY: she * (gy[0] + gx[1]),
            XZ: she * (gz[0] + gx[2]), YZ: she * (gz[1] + gy[2]),
        }
        for k, a in adds.items():
            spad[k, layer, pl.ds(8, 64), :] = spad[k, layer, pl.ds(8, 64), :] + a

    def send_rows(n, src, dst):
        def one(k, _):
            t = lax.rem(c + k, COLS)
            pltpu.make_async_remote_copy(
                src_ref=src(t), dst_ref=dst(c), send_sem=col_send.at[n],
                recv_sem=col_recv.at[n], device_id=(r, t), device_id_type=MESH,
            ).start()
            return 0

        lax.fori_loop(1, COLS, one, 0)
        own = pltpu.make_async_copy(src(c), dst(c), own_sem.at[n])
        own.start()
        return own

    def wait_rows(n, own, whole):
        copy = pltpu.make_async_remote_copy(
            src_ref=whole, dst_ref=whole, send_sem=col_send.at[n],
            recv_sem=col_recv.at[n], device_id=after, device_id_type=MESH,
        )
        copy.wait()
        own.wait()

    def four(t):
        return pl.ds(pl.multiple_of(4 * t, 4), 4)

    def send_top(n):
        return send_rows(
            n, lambda t: vpad.at[:, 0, pl.ds(pl.multiple_of(8 + 4 * t, 4), 4), :],
            lambda t: rows_in.at[n // 2, :, four(t), :],
        )

    def wait_top(n, own):
        wait_rows(n, own, rows_in.at[n // 2, :, pl.ds(0, 60), :])

    def send_traction(n, count):
        return send_rows(
            n, lambda t: rows_out.at[n // 2, pl.ds(0, count), four(t), :],
            lambda t: trac.at[n // 2, pl.ds(0, count), four(t), :],
        )

    def wait_traction(n, own, count):
        wait_rows(n, own, trac.at[n // 2, pl.ds(0, count), pl.ds(0, 60), :])

    def send_all(n, src, dst):
        def one(k, _):
            t = lax.rem(me + k, DEVS)
            pltpu.make_async_remote_copy(
                src_ref=src.at[t], dst_ref=dst.at[me], send_sem=all_send.at[n],
                recv_sem=all_recv.at[n], device_id=device(k), device_id_type=MESH,
            ).start()
            return 0

        lax.fori_loop(1, DEVS, one, 0)
        own = pltpu.make_async_copy(src.at[me], dst.at[me], own_sem.at[5 + n])
        own.start()
        return own

    def wait_all(n, own, dst):
        whole = dst.at[pl.ds(0, DEVS - 1)]
        copy = pltpu.make_async_remote_copy(
            src_ref=whole, dst_ref=whole, send_sem=all_send.at[n],
            recv_sem=all_recv.at[n], device_id=after, device_id_type=MESH,
        )
        copy.wait()
        own.wait()

    def turn(re, im, cos, sin, sign):
        return re * cos - im * (sign * sin), im * cos + re * (sign * sin)

    def to_send(blocks, sign, out):
        data = []
        for re, im in blocks:
            data.append(jnp.concatenate([re, -sign * im], axis=1))
            data.append(jnp.concatenate([im, sign * re], axis=1))
        hi, lo = halves(jnp.concatenate(data, axis=0))
        full = dot(left[...], jnp.concatenate([hi, lo, hi], axis=1), ((1,), (1,)))
        for i in range(len(blocks)):
            out[:, i, :] = full[:, 128 * i : 128 * i + 128]

    def from_recv(buf, which, sign):
        turned = [buf[:, i, :].T for i in which]
        hi, lo = halves(jnp.concatenate(turned, axis=0))
        full = dot(jnp.concatenate([hi, lo, hi], axis=1), right[...])
        result = []
        for i in range(len(turned)):
            a = full[128 * i : 128 * i + 128]
            p, q = a[:, :128], a[:, 128:]
            result.append((p[:64] - sign * q[64:], p[64:] + sign * q[:64]))
        return result

    def rows_forward(fields, out):
        hi, lo = halves(jnp.concatenate(fields, axis=1))
        mixed = dot(first[...], jnp.concatenate([hi, lo, hi, lo], axis=0))
        cos, sin = small[0:16][None], small[16:32][None]
        blocks = []
        for i in range(len(fields)):
            a = mixed[:, 128 * i : 128 * i + 128]
            re, im = a[:64].reshape(4, 16, 128), a[64:].reshape(4, 16, 128)
            re, im = turn(re, im, cos, sin, -1.0)
            blocks.append((re.reshape(64, 128), im.reshape(64, 128)))
        to_send(blocks, -1.0, out)

    def rows_inverse(buf, which):
        cos, sin = small[0:16][None], small[16:32][None]
        parts = []
        for re, im in from_recv(buf, which, 1.0):
            re, im = turn(re.reshape(4, 16, 128), im.reshape(4, 16, 128), cos, sin, 1.0)
            parts.append(
                jnp.concatenate([re.reshape(64, 128), im.reshape(64, 128)], axis=0)
            )
        hi, lo = halves(jnp.concatenate(parts, axis=1))
        full = dot(last[...], jnp.concatenate([hi, lo, hi], axis=0))
        return [full[:, 128 * i : 128 * i + 128] for i in range(len(parts))]

    def spectrum_forward(buf, step):
        for i, (re, im) in enumerate(from_recv(buf, (0, 1, 2), -1.0)):
            a = []
            for xl in range(4):
                cos, sin = small[32 + xl : 33 + xl], small[36 + xl : 37 + xl]
                b = re[16 * xl : 16 * xl + 16], im[16 * xl : 16 * xl + 16]
                a.append(b if xl == 0 else turn(*b, cos, sin, -1.0))
            for k, (zr, zi) in enumerate(quarter(a, -1.0)):
                spec[step, i, 0, :, 128 * k : 128 * k + 128] = zr
                spec[step, i, 1, :, 128 * k : 128 * k + 128] = zi

    def quarter(a, sign):
        (ar, ai), (br, bi), (cr, ci), (dr, di) = a
        pr, pi, mr, mi = ar + cr, ai + ci, ar - cr, ai - ci
        qr, qi, nr, ni = br + dr, bi + di, br - dr, bi - di
        tr, ti = -sign * ni, sign * nr
        return ((pr + qr, pi + qi), (mr + tr, mi + ti), (pr - qr, pi - qi), (mr - tr, mi - ti))

    def spectrum_inverse(loads_, out):
        blocks = []
        for re, im in loads_:
            a = [(re[:, 128 * k : 128 * k + 128], im[:, 128 * k : 128 * k + 128]) for k in range(4)]
            res, ims = [], []
            for xl, (zr, zi) in enumerate(quarter(a, 1.0)):
                if xl:
                    cos, sin = small[32 + xl : 33 + xl], small[36 + xl : 37 + xl]
                    zr, zi = turn(zr, zi, cos, sin, 1.0)
                res.append(zr)
                ims.append(zi)
            blocks.append((jnp.concatenate(res, axis=0), jnp.concatenate(ims, axis=0)))
        to_send(blocks, 1.0, out)

    def convolve_past(step):
        for i in range(3):
            def lag(m, acc):
                kr, ki = ker[m, i, 0].astype(F32), ker[m, i, 1].astype(F32)
                hr, hi = his[m - 1 - step, i, 0].astype(F32), his[m - 1 - step, i, 1].astype(F32)
                return acc[0] + (kr * hr - ki * hi), acc[1] + (kr * hi + ki * hr)

            zero = jnp.zeros((16, 512), F32)
            re, im = lax.fori_loop(1 + step, 12, lag, (zero, zero))
            part[step, i, 0], part[step, i, 1] = re, im

    def add_lag(i, m, step, re, im):
        kr, ki = ker[m, i, 0].astype(F32), ker[m, i, 1].astype(F32)
        sr, si = spec[step, i, 0], spec[step, i, 1]
        return re + (kr * sr - ki * si), im + (kr * si + ki * sr)

    for copy in stress_loads:
        copy.wait()
    halo = start_halo(0, spad, 3, stress_y)
    pl.semaphore_wait(barrier, DEVS - 1)
    for copy in halo:
        copy.start()
    for copy in coef_loads:
        copy.wait()
    own_b = send_rows(4, lambda t: coef.at[0, 0, four(t), :], lambda t: buo_rows.at[four(t), :])
    for copy in conv_loads:
        copy.wait()
    convolve_past(0)
    vel_load.wait()
    for copy in halo:
        copy.wait()
    both = edges_of(0)
    new_velocity(both, 0)
    own = send_top(0)
    for layer in range(1, 4):
        new_velocity(both, layer)
    halo = start_halo(1, vpad, 3, vel_y)
    for copy in halo:
        copy.start()
    for copy in table_loads:
        copy.wait()
    wait_top(0, own)
    rows_forward([rows_in[0, i] for i in range(3)], send_a.at[0])
    own = send_all(0, send_a.at[0], recv_a.at[0])

    for copy in coef_late:
        copy.wait()
    for copy in halo:
        copy.wait()
    both = edges_of(1)
    for layer in range(4):
        new_stress(both, layer)
    halo = start_halo(2, spad, 3, stress_y)
    for copy in halo:
        copy.start()

    wait_all(0, own, recv_a.at[0])
    spectrum_forward(recv_a.at[0], 0)
    now = [add_lag(i, 0, 0, part[0, i, 0], part[0, i, 1]) for i in range(3)]
    ax = [small[40 + k : 41 + k] for k in range(4)]
    ay = along[...]

    def slope(xs, ys):
        return jnp.concatenate(
            [
                ax[k] * xs[:, 128 * k : 128 * k + 128] + ay * ys[:, 128 * k : 128 * k + 128]
                for k in range(4)
            ],
            axis=1,
        )

    slopes = (-slope(now[0][1], now[1][1]), slope(now[0][0], now[1][0]))
    spectrum_inverse([*now, slopes], send_b.at[0])
    own = send_all(1, send_b.at[0], recv_b.at[0])

    for copy in halo:
        copy.wait()
    both = edges_of(2)
    new_velocity(both, 0)
    own_top = send_top(2)
    for layer in range(1, 4):
        new_velocity(both, layer)
    convolve_past(1)
    for i in range(3):
        re, im = add_lag(i, 1, 0, part[1, i, 0], part[1, i, 1])
        part[1, i, 0], part[1, i, 1] = re, im
    wait_rows(4, own_b, buo_rows.at[pl.ds(0, 60), :])
    wait_top(2, own_top)

    wait_all(1, own, recv_b.at[0])
    (slope_rows,) = rows_inverse(recv_b.at[0], (3,))
    rows_forward(
        [rows_in[1, 0], rows_in[1, 1], rows_in[1, 2] + buo_rows[...] * slope_rows], send_a.at[1]
    )
    own = send_all(2, send_a.at[1], recv_a.at[1])
    for i, t in enumerate(rows_inverse(recv_b.at[0], (0, 1, 2))):
        rows_out[0, i] = t
    rows_out[0, 3] = slope_rows
    own_trac = send_traction(1, 4)
    wait_traction(1, own_trac, 4)
    inner = pl.ds(8, 64)
    for i in range(3):
        t = trac[0, i]
        vpad[i, 1, inner, :] = vpad[i, 1, inner, :] - NEAR * (coef[0, 1] * t)
        vpad[i, 2, inner, :] = vpad[i, 2, inner, :] - FAR * (coef[0, 2] * t)
        k = (XZ, YZ, ZZ)[i]
        spad[k, 0, inner, :] = spad[k, 0, inner, :] + t
    vpad[2, 0, inner, :] = vpad[2, 0, inner, :] + coef[0, 0] * trac[0, 3]
    halo = start_halo(3, vpad, 3, vel_y)
    for copy in halo:
        copy.start()
    outs = [pltpu.make_async_copy(vpad.at[:, :, inner, :], vel_out, out_sem.at[0])]
    outs[-1].start()

    wait_all(2, own, recv_a.at[1])
    spectrum_forward(recv_a.at[1], 1)
    spectrum_inverse(
        [add_lag(i, 0, 1, part[1, i, 0], part[1, i, 1]) for i in range(3)], send_b.at[1]
    )
    own = send_all(3, send_b.at[1], recv_b.at[1])
    outs.append(pltpu.make_async_copy(spec, spe_out, out_sem.at[1]))
    outs[-1].start()

    for copy in halo:
        copy.wait()
    both = edges_of(3)
    for layer in range(4):
        new_stress(both, layer)
    for k in (XX, XY, YY):
        outs.append(
            pltpu.make_async_copy(
                spad.at[k, :, inner, :], str_out.at[PLACE[k]], out_sem.at[2 + k]
            )
        )
        outs[-1].start()
    wait_all(3, own, recv_b.at[1])
    for i, t in enumerate(rows_inverse(recv_b.at[1], (0, 1, 2))):
        rows_out[1, i] = t
    own_trac = send_traction(3, 3)
    wait_traction(3, own_trac, 3)
    for i, k in enumerate((XZ, YZ, ZZ)):
        spad[k, 0, inner, :] = spad[k, 0, inner, :] + trac[1, i]
        outs.append(
            pltpu.make_async_copy(
                spad.at[k, :, inner, :], str_out.at[PLACE[k]], out_sem.at[2 + k]
            )
        )
        outs[-1].start()
    for copy in outs:
        copy.wait()


def on_device(velocity, stress, buoyancy, lame, shear, kernel, history):
    left, right, first, last, small, along = (jnp.asarray(t) for t in tables())
    anyspace = pl.BlockSpec(memory_space=pl.ANY)
    vm, dma = pltpu.VMEM, pltpu.SemaphoreType.DMA
    return pl.pallas_call(
        kernel_body,
        out_shape=(
            jax.ShapeDtypeStruct(velocity.shape, F32),
            jax.ShapeDtypeStruct(stress.shape, F32),
            jax.ShapeDtypeStruct((2, 3, 2, 16, 512), F32),
        ),
        in_specs=[anyspace] * 13,
        out_specs=[anyspace] * 3,
        scratch_shapes=[
            vm((3, 4, 80, 128), F32),
            vm((6, 4, 80, 128), F32),
            vm((3, 4, 64, 128), F32),
            vm((12, 3, 2, 16, 512), BF16),
            vm((11, 3, 2, 16, 512), BF16),
            vm((128, 768), BF16),
            vm((384, 256), BF16),
            vm((128, 256), BF16),
            vm((64, 384), BF16),
            vm((48, 128), F32),
            vm((16, 128), F32),
            vm((4, 64, 128), F32),
            vm((4, 64, 128), F32),
            vm((4, 64, 128), F32),
            vm((2, 3, 64, 128), F32),
            vm((64, 128), F32),
            vm((2, 128, 3, 128), F32),
            vm((2, 128, 3, 128), F32),
            vm((2, 128, 4, 128), F32),
            vm((2, 128, 4, 128), F32),
            vm((2, 4, 64, 128), F32),
            vm((2, 4, 64, 128), F32),
            vm((2, 3, 2, 16, 512), F32),
            vm((2, 3, 2, 16, 512), F32),
            dma((18,)),
            dma((8,)),
            dma((4, 4)),
            dma((4, 4)),
            dma((5,)),
            dma((5,)),
            dma((4,)),
            dma((4,)),
            dma((9,)),
        ],
        compiler_params=pltpu.CompilerParams(
            collective_id=0, has_side_effects=True, vmem_limit_bytes=56 << 20
        ),
    )(
        velocity, stress, buoyancy, lame, shear, kernel, history,
        left, right, first, last, small, along,
    )


def solution(mesh):
    spread = P(None, None, None, ("row", "col"), None)
    return jax.shard_map(
        on_device,
        mesh=mesh,
        in_specs=(
            P(None, None, "row", "col"),
            P(None, None, "row", "col"),
            P(None, "row", "col"),
            P(None, "row", "col"),
            P(None, "row", "col"),
            spread,
            spread,
        ),
        out_specs=(P(None, None, "row", "col"), P(None, None, "row", "col"), spread),
        check_vma=False,
    )
```

```python
import math

import jax
import jax.numpy as jnp
import numpy as np
from jax import lax
from jax.experimental import pallas as pl
from jax.experimental.pallas import tpu as pltpu
from jax.sharding import PartitionSpec as P

MESH = pl.DeviceIdType.MESH
F32, BF16 = jnp.float32, jnp.bfloat16
ROWS, COLS, DEVS = 8, 16, 128
NEAR, FAR = 2.0 / 3.0, -1.0 / 12.0
PLACE = (0, 3, 4, 1, 5, 2)
XX, XY, XZ, YY, YZ, ZZ = range(6)


def tables():
    def halves(a):
        hi = a.astype(BF16)
        lo = (a - hi.astype(np.float64)).astype(BF16)
        return hi, lo

    i128 = np.arange(128)
    ang = 2 * np.pi * (np.outer(i128, i128) % 128) / 128
    cos, sin = np.cos(ang), np.sin(ang)
    hi, lo = halves(np.concatenate([cos, sin], axis=1))
    left = np.concatenate([hi, hi, lo], axis=1)
    right = np.concatenate([hi, hi, lo], axis=0)
    j, c = np.arange(16), np.arange(16)
    ang = 2 * np.pi * (np.outer(j, c) % 16) / 16
    one = np.zeros((2, 4, 16, 16, 4))
    for xl in range(4):
        one[0, xl, :, :, xl] = np.cos(ang)
        one[1, xl, :, :, xl] = -np.sin(ang)
    one = one.reshape(128, 64) / 1024.0
    hi, lo = halves(one)
    first = np.concatenate([hi, hi, lo, lo], axis=1)
    hi, lo = halves(one.T)
    last = np.concatenate([hi, hi, lo], axis=1)
    small = np.zeros((48, 128), np.float32)
    ang = 2 * np.pi * np.outer(j, i128) / 2048
    small[0:16], small[16:32] = np.cos(ang), np.sin(ang)
    ang = 2 * np.pi * np.outer(np.arange(4), i128) / 512
    small[32:36], small[36:40] = np.cos(ang), np.sin(ang)
    th = 2 * np.pi * np.arange(512) / 512
    small[40:44] = (4 / 3 * np.sin(th) - 1 / 6 * np.sin(2 * th)).reshape(4, 128)
    th = 2 * np.pi * np.arange(2048) / 2048
    along = (4 / 3 * np.sin(th) - 1 / 6 * np.sin(2 * th)).reshape(128, 16, 1)
    along = np.broadcast_to(along, (128, 16, 128)).astype(np.float32)
    return left, right, first, last, small, along


def far_first(count):
    ring = (0, 1, 2, 1)

    def way(k):
        row, col = k // COLS, k % COLS
        z = 2 * (col // 8) + row % 2
        return ring[row // 2] + ring[z] + ring[col // 2 % 4] + 0.1 * (col % 2)

    return sorted(range(1, count), key=way, reverse=True)


def halves(x):
    hi = x.astype(BF16)
    return hi, (x - hi.astype(F32)).astype(BF16)


def dot(a, b, contract=((1,), (0,))):
    return lax.dot_general(a, b, (contract, ((), ())), preferred_element_type=F32)


def kernel_body(
    vel_in, str_in, buo_in, lam_in, she_in, ker_in, his_in,
    left_in, right_in, first_in, last_in, small_in, along_in,
    vel_out, str_out, spec,
    vpad, spad, coef, ker, his, left, right, first, last, small, along,
    pack, pack_low, pack_high, rows_in, buo_rows, send_a, recv_a, send_b, recv_b, send_w, recv_w,
    rows_out, trac, part,
    in_sem, halo_send, halo_recv, col_send, col_recv, all_send, all_recv, own_sem, ready,
):
    r, c = lax.axis_index("row"), lax.axis_index("col")
    me = r * COLS + c

    def greet(semaphore, row, col):
        pl.semaphore_signal(semaphore, inc=1, device_id=(row, col), device_id_type=MESH)
        return 0

    barrier = pltpu.get_barrier_semaphore()
    lax.fori_loop(1, ROWS, lambda k, _: greet(barrier, lax.rem(r + k, ROWS), c), 0)
    lax.fori_loop(1, COLS, lambda k, _: greet(barrier, r, lax.rem(c + k, COLS)), 0)

    loads = []

    def load(src, dst):
        copy = pltpu.make_async_copy(src, dst, in_sem.at[len(loads)])
        copy.start()
        loads.append(copy)
        return copy

    stress_loads = [
        load(str_in.at[PLACE[k]], spad.at[k, :, pl.ds(8, 64), :]) for k in range(6)
    ]
    coef_loads = [load(buo_in, coef.at[0])]
    vel_load = load(vel_in, vpad.at[:, :, pl.ds(8, 64), :])
    conv_loads = [load(ker_in, ker), load(his_in, his)]
    table_loads = [
        load(left_in, left), load(right_in, right), load(first_in, first),
        load(last_in, last), load(small_in, small), load(along_in.at[me], along),
    ]
    coef_late = [load(lam_in, coef.at[1]), load(she_in, coef.at[2])]

    up, down = (lax.rem(r + 1, ROWS), c), (lax.rem(r + ROWS - 1, ROWS), c)
    after, before = (r, lax.rem(c + 1, COLS)), (r, lax.rem(c + COLS - 1, COLS))

    lane = lax.broadcasted_iota(jnp.int32, (64, 128), 1)
    edge = jnp.logical_or(lane < 2, lane >= 126)

    def start_halo(n, pad, comps, layers):
        packed = jnp.zeros((64, 128), F32)
        for k in range(3 * len(layers)):
            comp, layer = comps[k // len(layers)], layers[k % len(layers)]
            f = pad[comp, layer, pl.ds(8, 64), :]
            packed += pltpu.roll(jnp.where(edge, f, 0.0), 4 * k + 2, 1)
        pack[n] = packed

        def remote(i, src, dst, to):
            copy = pltpu.make_async_remote_copy(
                src_ref=src, dst_ref=dst, send_sem=halo_send.at[n, i],
                recv_sem=halo_recv.at[n, i], device_id=to, device_id_type=MESH,
            )
            return copy

        some = pl.ds(layers[0], len(layers))
        copies = [
            remote(0, pad.at[pl.ds(0, 3), some, pl.ds(64, 8), :],
                   pad.at[pl.ds(0, 3), some, pl.ds(0, 8), :], up),
            remote(1, pad.at[pl.ds(0, 3), some, pl.ds(8, 8), :],
                   pad.at[pl.ds(0, 3), some, pl.ds(72, 8), :], down),
            remote(2, pack.at[n], pack_low.at[n], after),
            remote(3, pack.at[n], pack_high.at[n], before),
        ]
        for copy in copies:
            copy.start()
        return copies

    def edges_of(n):
        return jnp.where(lax.rem(lane, 4) >= 2, pack_high[n], pack_low[n])

    def dx(pad, comp, layer):
        def at(o):
            return pad[comp, layer, pl.ds(8 + o, 64), :]

        return NEAR * (at(1) - at(-1)) + FAR * (at(2) - at(-2))

    def dy(f, both, k):
        e = pltpu.roll(both, 128 - (4 * k + 2), 1)
        p1 = pltpu.roll(jnp.where(lane == 0, e, f), 127, 1)
        p2 = pltpu.roll(jnp.where(lane < 2, e, f), 126, 1)
        m1 = pltpu.roll(jnp.where(lane == 127, e, f), 1, 1)
        m2 = pltpu.roll(jnp.where(lane >= 126, e, f), 2, 1)
        return NEAR * (p1 - m1) + FAR * (p2 - m2)

    def dz(pad, comp, layer):
        total = None
        for o, w in ((1, NEAR), (-1, -NEAR), (2, FAR), (-2, -FAR)):
            if 0 <= layer + o < 4:
                term = w * pad[comp, layer + o, pl.ds(8, 64), :]
                total = term if total is None else total + term
        return total

    stress_y, vel_y = (XY, YY, YZ), (0, 1, 2)
    top, deep, deep4 = (0,), (1, 2, 3), (0, 1, 2, 3)

    def new_velocity(both, layers, layer):
        along_x = [dx(spad, k, layer) for k in (XX, XY, XZ)]
        along_y = [
            dy(spad[k, layer, pl.ds(8, 64), :], both, len(layers) * i + layer - layers[0])
            for i, k in enumerate((XY, YY, YZ))
        ]
        along_z = [dz(spad, k, layer) for k in (XZ, YZ, ZZ)]
        b = coef[0, layer]
        for i in range(3):
            vpad[i, layer, pl.ds(8, 64), :] = vpad[i, layer, pl.ds(8, 64), :] + b * (
                along_x[i] + along_y[i] + along_z[i]
            )

    def new_stress(both, layer, out=None):
        gx = [dx(vpad, i, layer) for i in range(3)]
        gy = [dy(vpad[i, layer, pl.ds(8, 64), :], both, 4 * i + layer) for i in range(3)]
        gz = [dz(vpad, i, layer) for i in range(3)]
        lam, she = coef[1, layer], coef[2, layer]
        spread = lam * (gx[0] + gy[1] + gz[2])
        adds = {
            XX: spread + 2.0 * she * gx[0], YY: spread + 2.0 * she * gy[1],
            ZZ: spread + 2.0 * she * gz[2], XY: she * (gy[0] + gx[1]),
            XZ: she * (gz[0] + gx[2]), YZ: she * (gz[1] + gy[2]),
        }
        for k, a in adds.items():
            total = spad[k, layer, pl.ds(8, 64), :] + a
            if out is None:
                spad[k, layer, pl.ds(8, 64), :] = total
            else:
                out[PLACE[k], layer] = total

    def send_rows(n, src, dst):
        for k in far_first(COLS):
            t = c ^ k
            pltpu.make_async_remote_copy(
                src_ref=src(t), dst_ref=dst(c), send_sem=col_send.at[n],
                recv_sem=col_recv.at[n], device_id=(r, t), device_id_type=MESH,
            ).start()
        own = pltpu.make_async_copy(src(c), dst(c), own_sem.at[n])
        own.start()
        return own

    def wait_rows(n, own, whole):
        copy = pltpu.make_async_remote_copy(
            src_ref=whole, dst_ref=whole, send_sem=col_send.at[n],
            recv_sem=col_recv.at[n], device_id=after, device_id_type=MESH,
        )
        copy.wait()
        own.wait()

    def four(t):
        return pl.ds(pl.multiple_of(4 * t, 4), 4)

    def send_top(n):
        return send_rows(
            n, lambda t: vpad.at[:, 0, pl.ds(pl.multiple_of(8 + 4 * t, 4), 4), :],
            lambda t: rows_in.at[n // 2, :, four(t), :],
        )

    def wait_top(n, own):
        wait_rows(n, own, rows_in.at[n // 2, :, pl.ds(0, 60), :])

    def send_traction(n, count):
        return send_rows(
            n, lambda t: rows_out.at[n // 2, pl.ds(0, count), four(t), :],
            lambda t: trac.at[n // 2, pl.ds(0, count), four(t), :],
        )

    def wait_traction(n, own, count):
        wait_rows(n, own, trac.at[n // 2, pl.ds(0, count), pl.ds(0, 60), :])

    def send_all(n, src, dst):
        for k in far_first(DEVS):
            pltpu.make_async_remote_copy(
                src_ref=src.at[me ^ k], dst_ref=dst.at[me], send_sem=all_send.at[n],
                recv_sem=all_recv.at[n], device_id=(r ^ (k // COLS), c ^ (k % COLS)),
                device_id_type=MESH,
            ).start()
        own = pltpu.make_async_copy(src.at[me], dst.at[me], own_sem.at[5 + n])
        own.start()
        return own

    def wait_all(n, own, dst):
        whole = dst.at[pl.ds(0, DEVS - 1)]
        copy = pltpu.make_async_remote_copy(
            src_ref=whole, dst_ref=whole, send_sem=all_send.at[n],
            recv_sem=all_recv.at[n], device_id=after, device_id_type=MESH,
        )
        copy.wait()
        own.wait()

    def turn(re, im, cos, sin, sign):
        return re * cos - im * (sign * sin), im * cos + re * (sign * sin)

    def to_send(blocks, sign, out):
        data = []
        for re, im in blocks:
            data.append(jnp.concatenate([re, -sign * im], axis=1))
            data.append(jnp.concatenate([im, sign * re], axis=1))
        hi, lo = halves(jnp.concatenate(data, axis=0))
        full = dot(left[...], jnp.concatenate([hi, lo, hi], axis=1), ((1,), (1,)))
        for i in range(len(blocks)):
            out[:, i, :] = full[:, 128 * i : 128 * i + 128]

    def from_recv(buf, which, sign):
        turned = [buf[:, i, :].T for i in which]
        hi, lo = halves(jnp.concatenate(turned, axis=0))
        full = dot(jnp.concatenate([hi, lo, hi], axis=1), right[...])
        result = []
        for i in range(len(turned)):
            a = full[128 * i : 128 * i + 128]
            p, q = a[:, :128], a[:, 128:]
            result.append((p[:64] - sign * q[64:], p[64:] + sign * q[:64]))
        return result

    def rows_forward(fields, out):
        hi, lo = halves(jnp.concatenate(fields, axis=1))
        mixed = dot(first[...], jnp.concatenate([hi, lo, hi, lo], axis=0))
        cos, sin = small[0:16][None], small[16:32][None]
        blocks = []
        for i in range(len(fields)):
            a = mixed[:, 128 * i : 128 * i + 128]
            re, im = a[:64].reshape(4, 16, 128), a[64:].reshape(4, 16, 128)
            re, im = turn(re, im, cos, sin, -1.0)
            blocks.append((re.reshape(64, 128), im.reshape(64, 128)))
        to_send(blocks, -1.0, out)

    def rows_inverse(buf, which):
        cos, sin = small[0:16][None], small[16:32][None]
        parts = []
        for re, im in from_recv(buf, which, 1.0):
            re, im = turn(re.reshape(4, 16, 128), im.reshape(4, 16, 128), cos, sin, 1.0)
            parts.append(
                jnp.concatenate([re.reshape(64, 128), im.reshape(64, 128)], axis=0)
            )
        hi, lo = halves(jnp.concatenate(parts, axis=1))
        full = dot(last[...], jnp.concatenate([hi, lo, hi], axis=0))
        return [full[:, 128 * i : 128 * i + 128] for i in range(len(parts))]

    def spectrum_forward(buf, step):
        for i, (re, im) in enumerate(from_recv(buf, (0, 1, 2), -1.0)):
            a = []
            for xl in range(4):
                cos, sin = small[32 + xl : 33 + xl], small[36 + xl : 37 + xl]
                b = re[16 * xl : 16 * xl + 16], im[16 * xl : 16 * xl + 16]
                a.append(b if xl == 0 else turn(*b, cos, sin, -1.0))
            for k, (zr, zi) in enumerate(quarter(a, -1.0)):
                spec[step, i, 0, :, 128 * k : 128 * k + 128] = zr
                spec[step, i, 1, :, 128 * k : 128 * k + 128] = zi

    def quarter(a, sign):
        (ar, ai), (br, bi), (cr, ci), (dr, di) = a
        pr, pi, mr, mi = ar + cr, ai + ci, ar - cr, ai - ci
        qr, qi, nr, ni = br + dr, bi + di, br - dr, bi - di
        tr, ti = -sign * ni, sign * nr
        return ((pr + qr, pi + qi), (mr + tr, mi + ti), (pr - qr, pi - qi), (mr - tr, mi - ti))

    def spectrum_inverse(loads_, out):
        blocks = []
        for re, im in loads_:
            a = [(re[:, 128 * k : 128 * k + 128], im[:, 128 * k : 128 * k + 128]) for k in range(4)]
            res, ims = [], []
            for xl, (zr, zi) in enumerate(quarter(a, 1.0)):
                if xl:
                    cos, sin = small[32 + xl : 33 + xl], small[36 + xl : 37 + xl]
                    zr, zi = turn(zr, zi, cos, sin, 1.0)
                res.append(zr)
                ims.append(zi)
            blocks.append((jnp.concatenate(res, axis=0), jnp.concatenate(ims, axis=0)))
        to_send(blocks, 1.0, out)

    def convolve_past(step):
        for i in range(3):
            def lag(m, acc):
                kr, ki = ker[m, i, 0].astype(F32), ker[m, i, 1].astype(F32)
                hr, hi = his[m - 1 - step, i, 0].astype(F32), his[m - 1 - step, i, 1].astype(F32)
                return acc[0] + (kr * hr - ki * hi), acc[1] + (kr * hi + ki * hr)

            zero = jnp.zeros((16, 512), F32)
            re, im = lax.fori_loop(1 + step, 12, lag, (zero, zero))
            part[step, i, 0], part[step, i, 1] = re, im

    def add_lag(i, m, step, re, im):
        kr, ki = ker[m, i, 0].astype(F32), ker[m, i, 1].astype(F32)
        sr, si = spec[step, i, 0], spec[step, i, 1]
        return re + (kr * sr - ki * si), im + (kr * si + ki * sr)

    def finish(copies):
        for copy in copies:
            copy.wait()

    finish(stress_loads)
    pl.semaphore_wait(barrier, ROWS + COLS - 2)
    halo_top = start_halo(0, spad, stress_y, top)
    lax.fori_loop(1, COLS, lambda k, _: greet(ready, r, lax.rem(c + k, COLS)), 0)
    halo_deep = start_halo(1, spad, stress_y, deep)
    finish(coef_loads)
    own_b = send_rows(4, lambda t: coef.at[0, 0, four(t), :], lambda t: buo_rows.at[four(t), :])
    finish(conv_loads)
    convolve_past(0)
    vel_load.wait()
    finish(halo_top)
    new_velocity(edges_of(0), top, 0)
    own = send_top(0)
    finish(halo_deep)
    both = edges_of(1)
    for layer in deep:
        new_velocity(both, deep, layer)
    halo = start_halo(2, vpad, vel_y, deep4)
    convolve_past(1)
    finish(table_loads)
    wait_top(0, own)
    rows_forward([rows_in[0, i] for i in range(3)], send_a.at[0])
    pl.semaphore_wait(ready, COLS - 1)
    own = send_all(0, send_a.at[0], recv_a.at[0])

    finish(coef_late)
    finish(halo)
    both = edges_of(2)
    new_stress(both, 0)
    halo_top = start_halo(3, spad, stress_y, top)
    for layer in deep:
        new_stress(both, layer)
    halo_deep = start_halo(4, spad, stress_y, deep)

    wait_all(0, own, recv_a.at[0])
    spectrum_forward(recv_a.at[0], 0)
    now = [add_lag(i, 0, 0, part[0, i, 0], part[0, i, 1]) for i in range(3)]
    ax = [small[40 + k : 41 + k] for k in range(4)]
    ay = along[...]

    def slope(xs, ys):
        return jnp.concatenate(
            [
                ax[k] * xs[:, 128 * k : 128 * k + 128] + ay * ys[:, 128 * k : 128 * k + 128]
                for k in range(4)
            ],
            axis=1,
        )

    slopes = (-slope(now[0][1], now[1][1]), slope(now[0][0], now[1][0]))
    spectrum_inverse([slopes], send_w)

    finish(halo_top)
    new_velocity(edges_of(3), top, 0)
    own_top = send_top(2)
    own = send_all(1, send_w, recv_w)
    spectrum_inverse(now, send_b.at[0])
    own_t = send_all(4, send_b.at[0], recv_b.at[0])
    wait_rows(4, own_b, buo_rows.at[pl.ds(0, 60), :])
    wait_top(2, own_top)

    wait_all(1, own, recv_w)
    (slope_rows,) = rows_inverse(recv_w, (0,))
    rows_forward(
        [rows_in[1, 0], rows_in[1, 1], rows_in[1, 2] + buo_rows[...] * slope_rows], send_a.at[1]
    )
    own = send_all(2, send_a.at[1], recv_a.at[1])

    wait_all(4, own_t, recv_b.at[0])
    for i, t in enumerate(rows_inverse(recv_b.at[0], (0, 1, 2))):
        rows_out[0, i] = t
    rows_out[0, 3] = slope_rows
    own_trac = send_traction(1, 4)
    finish(halo_deep)
    both = edges_of(4)
    for layer in deep:
        new_velocity(both, deep, layer)
    for i in range(3):
        re, im = add_lag(i, 1, 0, part[1, i, 0], part[1, i, 1])
        part[1, i, 0], part[1, i, 1] = re, im

    wait_all(2, own, recv_a.at[1])
    spectrum_forward(recv_a.at[1], 1)
    spectrum_inverse(
        [add_lag(i, 0, 1, part[1, i, 0], part[1, i, 1]) for i in range(3)], send_b.at[1]
    )
    own = send_all(3, send_b.at[1], recv_b.at[1])

    wait_traction(1, own_trac, 4)
    inner = pl.ds(8, 64)
    for i in range(3):
        t = trac[0, i]
        vpad[i, 1, inner, :] = vpad[i, 1, inner, :] - NEAR * (coef[0, 1] * t)
        vpad[i, 2, inner, :] = vpad[i, 2, inner, :] - FAR * (coef[0, 2] * t)
        k = (XZ, YZ, ZZ)[i]
        spad[k, 0, inner, :] = spad[k, 0, inner, :] + t
    vpad[2, 0, inner, :] = vpad[2, 0, inner, :] + coef[0, 0] * trac[0, 3]
    halo = start_halo(5, vpad, vel_y, deep4)
    for i in range(3):
        for layer in range(4):
            vel_out[i, layer] = vpad[i, layer, inner, :]

    wait_all(3, own, recv_b.at[1])
    for i, t in enumerate(rows_inverse(recv_b.at[1], (0, 1, 2))):
        rows_out[1, i] = t
    own_trac = send_traction(3, 3)
    finish(halo)
    both = edges_of(5)
    for layer in range(4):
        new_stress(both, layer, str_out)
    wait_traction(3, own_trac, 3)
    for i, k in enumerate((XZ, YZ, ZZ)):
        str_out[PLACE[k], 0] = str_out[PLACE[k], 0] + trac[1, i]


def store_body(*refs):
    half = len(refs) // 2
    copies = [
        pltpu.make_async_copy(refs[i], refs[half + i], refs[-1].at[i]) for i in range(half)
    ]
    for copy in copies:
        copy.start()
    for copy in copies:
        copy.wait()


def on_device(velocity, stress, buoyancy, lame, shear, kernel, history):
    left, right, first, last, small, along = (jnp.asarray(t) for t in tables())
    anyspace = pl.BlockSpec(memory_space=pl.ANY)
    vm, dma = pltpu.VMEM, pltpu.SemaphoreType.DMA
    shapes = (
        jax.ShapeDtypeStruct(velocity.shape, F32),
        jax.ShapeDtypeStruct(stress.shape, F32),
        jax.ShapeDtypeStruct((2, 3, 2, 16, 512), F32),
    )
    results = pl.pallas_call(
        kernel_body,
        out_shape=tuple(vm(s.shape, s.dtype) for s in shapes),
        in_specs=[anyspace] * 13,
        out_specs=[pl.BlockSpec(memory_space=pltpu.VMEM)] * 3,
        scratch_shapes=[
            vm((3, 4, 80, 128), F32),
            vm((6, 4, 80, 128), F32),
            vm((3, 4, 64, 128), F32),
            vm((12, 3, 2, 16, 512), BF16),
            vm((11, 3, 2, 16, 512), BF16),
            vm((128, 768), BF16),
            vm((384, 256), BF16),
            vm((128, 256), BF16),
            vm((64, 384), BF16),
            vm((48, 128), F32),
            vm((16, 128), F32),
            vm((6, 64, 128), F32),
            vm((6, 64, 128), F32),
            vm((6, 64, 128), F32),
            vm((2, 3, 64, 128), F32),
            vm((64, 128), F32),
            vm((2, 128, 3, 128), F32),
            vm((2, 128, 3, 128), F32),
            vm((2, 128, 3, 128), F32),
            vm((2, 128, 3, 128), F32),
            vm((128, 1, 128), F32),
            vm((128, 1, 128), F32),
            vm((2, 4, 64, 128), F32),
            vm((2, 4, 64, 128), F32),
            vm((2, 3, 2, 16, 512), F32),
            dma((18,)),
            dma((6, 4)),
            dma((6, 4)),
            dma((5,)),
            dma((5,)),
            dma((5,)),
            dma((5,)),
            dma((10,)),
            pltpu.SemaphoreType.REGULAR,
        ],
        compiler_params=pltpu.CompilerParams(
            collective_id=0, has_side_effects=True, vmem_limit_bytes=56 << 20
        ),
    )(
        velocity, stress, buoyancy, lame, shear, kernel, history,
        left, right, first, last, small, along,
    )
    return pl.pallas_call(
        store_body,
        out_shape=shapes,
        in_specs=[anyspace] * 3,
        out_specs=[anyspace] * 3,
        scratch_shapes=[dma((3,))],
        compiler_params=pltpu.CompilerParams(vmem_limit_bytes=1 << 20),
    )(*results)


def solution(mesh):
    spread = P(None, None, None, ("row", "col"), None)
    return jax.shard_map(
        on_device,
        mesh=mesh,
        in_specs=(
            P(None, None, "row", "col"),
            P(None, None, "row", "col"),
            P(None, "row", "col"),
            P(None, "row", "col"),
            P(None, "row", "col"),
            spread,
            spread,
        ),
        out_specs=(P(None, None, "row", "col"), P(None, None, "row", "col"), spread),
        check_vma=False,
    )
```

```python
import math

import jax
import jax.numpy as jnp
import numpy as np
from jax import lax
from jax.experimental import pallas as pl
from jax.experimental.pallas import tpu as pltpu
from jax.sharding import PartitionSpec as P

MESH = pl.DeviceIdType.MESH
F32, BF16 = jnp.float32, jnp.bfloat16
ROWS, COLS, DEVS = 8, 16, 128
NEAR, FAR = 2.0 / 3.0, -1.0 / 12.0
PLACE = (0, 3, 4, 1, 5, 2)
XX, XY, XZ, YY, YZ, ZZ = range(6)


def tables():
    def halves(a):
        hi = a.astype(BF16)
        lo = (a - hi.astype(np.float64)).astype(BF16)
        return hi, lo

    i128 = np.arange(128)
    ang = 2 * np.pi * (np.outer(i128, i128) % 128) / 128
    cos, sin = np.cos(ang), np.sin(ang)
    hi, lo = halves(np.concatenate([cos, sin], axis=1))
    left = np.concatenate([hi, hi, lo], axis=1)
    right = np.concatenate([hi, hi, lo], axis=0)
    j, c = np.arange(16), np.arange(16)
    ang = 2 * np.pi * (np.outer(j, c) % 16) / 16
    one = np.zeros((2, 4, 16, 16, 4))
    for xl in range(4):
        one[0, xl, :, :, xl] = np.cos(ang)
        one[1, xl, :, :, xl] = -np.sin(ang)
    one = one.reshape(128, 64) / 1024.0
    hi, lo = halves(one)
    first = np.concatenate([hi, hi, lo, lo], axis=1)
    hi, lo = halves(one.T)
    last = np.concatenate([hi, hi, lo], axis=1)
    small = np.zeros((48, 128), np.float32)
    ang = 2 * np.pi * np.outer(j, i128) / 2048
    small[0:16], small[16:32] = np.cos(ang), np.sin(ang)
    ang = 2 * np.pi * np.outer(np.arange(4), i128) / 512
    small[32:36], small[36:40] = np.cos(ang), np.sin(ang)
    th = 2 * np.pi * np.arange(512) / 512
    small[40:44] = (4 / 3 * np.sin(th) - 1 / 6 * np.sin(2 * th)).reshape(4, 128)
    th = 2 * np.pi * np.arange(2048) / 2048
    along = (4 / 3 * np.sin(th) - 1 / 6 * np.sin(2 * th)).reshape(128, 16, 1)
    along = np.broadcast_to(along, (128, 16, 128)).astype(np.float32)
    return left, right, first, last, small, along


def far_first(count):
    ring = (0, 1, 2, 1)

    def way(k):
        row, col = k // COLS, k % COLS
        z = 2 * (col // 8) + row % 2
        return ring[row // 2] + ring[z] + ring[col // 2 % 4] + 0.1 * (col % 2)

    return sorted(range(1, count), key=way, reverse=True)


def halves(x):
    hi = x.astype(BF16)
    return hi, (x - hi.astype(F32)).astype(BF16)


def dot(a, b, contract=((1,), (0,))):
    return lax.dot_general(a, b, (contract, ((), ())), preferred_element_type=F32)


def kernel_body(
    vel_in, str_in, buo_in, lam_in, she_in, ker_in, his_in,
    left_in, right_in, first_in, last_in, small_in, along_in,
    vel_out, str_out, spec,
    vpad, spad, coef, ker, his, left, right, first, last, small, along,
    pack, pack_low, pack_high, rows_in, buo_rows, send_a, recv_a, send_b, recv_b, send_w, recv_w,
    rows_out, trac, part,
    in_sem, halo_send, halo_recv, col_send, col_recv, all_send, all_recv, own_sem, ready_z, ready_y,
):
    r, c = lax.axis_index("row"), lax.axis_index("col")
    me = r * COLS + c

    def greet(semaphore, row, col):
        pl.semaphore_signal(semaphore, inc=1, device_id=(row, col), device_id_type=MESH)

    up, down = (lax.rem(r + 1, ROWS), c), (lax.rem(r + ROWS - 1, ROWS), c)
    after, before = (r, lax.rem(c + 1, COLS)), (r, lax.rem(c + COLS - 1, COLS))
    along_z = [(r, c ^ 8), (r ^ 1, c), (r ^ 1, c ^ 8)]
    along_y = [(r ^ 4, c), (r ^ 2, c), (r ^ 6, c)]
    along_x = [(r, c ^ k) for k in (5, 4, 7, 6, 3, 2, 1)]
    near = [after, before, up, down, *along_y, *along_z, *along_x]

    barrier = pltpu.get_barrier_semaphore()
    for mate in near:
        greet(barrier, *mate)
    loads = []

    def load(src, dst):
        copy = pltpu.make_async_copy(src, dst, in_sem.at[len(loads)])
        copy.start()
        loads.append(copy)
        return copy

    stress_loads = [
        load(str_in.at[PLACE[k]], spad.at[k, :, pl.ds(8, 64), :]) for k in range(6)
    ]
    coef_loads = [load(buo_in, coef.at[0])]
    vel_load = load(vel_in, vpad.at[:, :, pl.ds(8, 64), :])
    conv_loads = [load(ker_in, ker), load(his_in, his)]
    table_loads = [
        load(left_in, left), load(right_in, right), load(first_in, first),
        load(last_in, last), load(small_in, small), load(along_in.at[me], along),
    ]
    coef_late = [load(lam_in, coef.at[1]), load(she_in, coef.at[2])]

    lane = lax.broadcasted_iota(jnp.int32, (64, 128), 1)
    edge = jnp.logical_or(lane < 2, lane >= 126)

    def make_halo(n, pad, comps, layers):
        packed = jnp.zeros((64, 128), F32)
        for k in range(3 * len(layers)):
            comp, layer = comps[k // len(layers)], layers[k % len(layers)]
            f = pad[comp, layer, pl.ds(8, 64), :]
            packed += pltpu.roll(jnp.where(edge, f, 0.0), 4 * k + 2, 1)
        pack[n] = packed

        def remote(i, src, dst, to):
            copy = pltpu.make_async_remote_copy(
                src_ref=src, dst_ref=dst, send_sem=halo_send.at[n, i],
                recv_sem=halo_recv.at[n, i], device_id=to, device_id_type=MESH,
            )
            return copy

        some = pl.ds(layers[0], len(layers))
        copies = [
            remote(0, pad.at[pl.ds(0, 3), some, pl.ds(64, 8), :],
                   pad.at[pl.ds(0, 3), some, pl.ds(0, 8), :], up),
            remote(1, pad.at[pl.ds(0, 3), some, pl.ds(8, 8), :],
                   pad.at[pl.ds(0, 3), some, pl.ds(72, 8), :], down),
            remote(2, pack.at[n], pack_low.at[n], after),
            remote(3, pack.at[n], pack_high.at[n], before),
        ]
        return copies

    def begin(copies):
        for copy in copies:
            copy.start()

    def start_halo(n, pad, comps, layers):
        copies = make_halo(n, pad, comps, layers)
        begin(copies)
        return copies

    def edges_of(n):
        return jnp.where(lax.rem(lane, 4) >= 2, pack_high[n], pack_low[n])

    def dx(pad, comp, layer):
        def at(o):
            return pad[comp, layer, pl.ds(8 + o, 64), :]

        return NEAR * (at(1) - at(-1)) + FAR * (at(2) - at(-2))

    def dy(f, both, k):
        e = pltpu.roll(both, 128 - (4 * k + 2), 1)
        p1 = pltpu.roll(jnp.where(lane == 0, e, f), 127, 1)
        p2 = pltpu.roll(jnp.where(lane < 2, e, f), 126, 1)
        m1 = pltpu.roll(jnp.where(lane == 127, e, f), 1, 1)
        m2 = pltpu.roll(jnp.where(lane >= 126, e, f), 2, 1)
        return NEAR * (p1 - m1) + FAR * (p2 - m2)

    def dz(pad, comp, layer):
        total = None
        for o, w in ((1, NEAR), (-1, -NEAR), (2, FAR), (-2, -FAR)):
            if 0 <= layer + o < 4:
                term = w * pad[comp, layer + o, pl.ds(8, 64), :]
                total = term if total is None else total + term
        return total

    stress_y, vel_y = (XY, YY, YZ), (0, 1, 2)
    top, deep, deep4 = (0,), (1, 2, 3), (0, 1, 2, 3)

    def new_velocity(both, layers, layer):
        along_x = [dx(spad, k, layer) for k in (XX, XY, XZ)]
        along_y = [
            dy(spad[k, layer, pl.ds(8, 64), :], both, len(layers) * i + layer - layers[0])
            for i, k in enumerate((XY, YY, YZ))
        ]
        along_z = [dz(spad, k, layer) for k in (XZ, YZ, ZZ)]
        b = coef[0, layer]
        for i in range(3):
            vpad[i, layer, pl.ds(8, 64), :] = vpad[i, layer, pl.ds(8, 64), :] + b * (
                along_x[i] + along_y[i] + along_z[i]
            )

    def new_stress(both, layer, out=None):
        gx = [dx(vpad, i, layer) for i in range(3)]
        gy = [dy(vpad[i, layer, pl.ds(8, 64), :], both, 4 * i + layer) for i in range(3)]
        gz = [dz(vpad, i, layer) for i in range(3)]
        lam, she = coef[1, layer], coef[2, layer]
        spread = lam * (gx[0] + gy[1] + gz[2])
        adds = {
            XX: spread + 2.0 * she * gx[0], YY: spread + 2.0 * she * gy[1],
            ZZ: spread + 2.0 * she * gz[2], XY: she * (gy[0] + gx[1]),
            XZ: she * (gz[0] + gx[2]), YZ: she * (gz[1] + gy[2]),
        }
        for k, a in adds.items():
            total = spad[k, layer, pl.ds(8, 64), :] + a
            if out is None:
                spad[k, layer, pl.ds(8, 64), :] = total
            else:
                out[PLACE[k], layer] = total

    def send_rows(n, src, dst):
        for k in far_first(COLS):
            t = c ^ k
            pltpu.make_async_remote_copy(
                src_ref=src(t), dst_ref=dst(c), send_sem=col_send.at[n],
                recv_sem=col_recv.at[n], device_id=(r, t), device_id_type=MESH,
            ).start()
        own = pltpu.make_async_copy(src(c), dst(c), own_sem.at[n])
        own.start()
        return own

    def wait_rows(n, own, whole):
        copy = pltpu.make_async_remote_copy(
            src_ref=whole, dst_ref=whole, send_sem=col_send.at[n],
            recv_sem=col_recv.at[n], device_id=after, device_id_type=MESH,
        )
        copy.wait()
        own.wait()

    def four(t):
        return pl.ds(pl.multiple_of(4 * t, 4), 4)

    def send_top(n):
        return send_rows(
            n, lambda t: vpad.at[:, 0, pl.ds(pl.multiple_of(8 + 4 * t, 4), 4), :],
            lambda t: rows_in.at[n // 2, :, four(t), :],
        )

    def wait_top(n, own):
        wait_rows(n, own, rows_in.at[n // 2, :, pl.ds(0, 60), :])

    def send_traction(n, count):
        return send_rows(
            n, lambda t: rows_out.at[n // 2, pl.ds(0, count), four(t), :],
            lambda t: trac.at[n // 2, pl.ds(0, count), four(t), :],
        )

    def wait_traction(n, own, count):
        wait_rows(n, own, trac.at[n // 2, pl.ds(0, count), pl.ds(0, 60), :])

    order = far_first(DEVS)

    def send_all(n, src, dst, some=order):
        for k in some:
            pltpu.make_async_remote_copy(
                src_ref=src.at[me ^ k], dst_ref=dst.at[me], send_sem=all_send.at[n],
                recv_sem=all_recv.at[n], device_id=(r ^ (k // COLS), c ^ (k % COLS)),
                device_id_type=MESH,
            ).start()
        if some[-1] != order[-1]:
            return None
        own = pltpu.make_async_copy(src.at[me], dst.at[me], own_sem.at[5 + n])
        own.start()
        return own

    def wait_all(n, own, dst):
        whole = dst.at[pl.ds(0, DEVS - 1)]
        copy = pltpu.make_async_remote_copy(
            src_ref=whole, dst_ref=whole, send_sem=all_send.at[n],
            recv_sem=all_recv.at[n], device_id=after, device_id_type=MESH,
        )
        copy.wait()
        own.wait()

    def turn(re, im, cos, sin, sign):
        return re * cos - im * (sign * sin), im * cos + re * (sign * sin)

    def to_send(blocks, sign, out):
        data = []
        for re, im in blocks:
            data.append(jnp.concatenate([re, -sign * im], axis=1))
            data.append(jnp.concatenate([im, sign * re], axis=1))
        hi, lo = halves(jnp.concatenate(data, axis=0))
        full = dot(left[...], jnp.concatenate([hi, lo, hi], axis=1), ((1,), (1,)))
        for i in range(len(blocks)):
            out[:, i, :] = full[:, 128 * i : 128 * i + 128]

    def from_recv(buf, which, sign):
        turned = [buf[:, i, :].T for i in which]
        hi, lo = halves(jnp.concatenate(turned, axis=0))
        full = dot(jnp.concatenate([hi, lo, hi], axis=1), right[...])
        result = []
        for i in range(len(turned)):
            a = full[128 * i : 128 * i + 128]
            p, q = a[:, :128], a[:, 128:]
            result.append((p[:64] - sign * q[64:], p[64:] + sign * q[:64]))
        return result

    def rows_forward(fields, out):
        hi, lo = halves(jnp.concatenate(fields, axis=1))
        mixed = dot(first[...], jnp.concatenate([hi, lo, hi, lo], axis=0))
        cos, sin = small[0:16][None], small[16:32][None]
        blocks = []
        for i in range(len(fields)):
            a = mixed[:, 128 * i : 128 * i + 128]
            re, im = a[:64].reshape(4, 16, 128), a[64:].reshape(4, 16, 128)
            re, im = turn(re, im, cos, sin, -1.0)
            blocks.append((re.reshape(64, 128), im.reshape(64, 128)))
        to_send(blocks, -1.0, out)

    def rows_inverse(buf, which):
        cos, sin = small[0:16][None], small[16:32][None]
        parts = []
        for re, im in from_recv(buf, which, 1.0):
            re, im = turn(re.reshape(4, 16, 128), im.reshape(4, 16, 128), cos, sin, 1.0)
            parts.append(
                jnp.concatenate([re.reshape(64, 128), im.reshape(64, 128)], axis=0)
            )
        hi, lo = halves(jnp.concatenate(parts, axis=1))
        full = dot(last[...], jnp.concatenate([hi, lo, hi], axis=0))
        return [full[:, 128 * i : 128 * i + 128] for i in range(len(parts))]

    def spectrum_forward(buf, step):
        for i, (re, im) in enumerate(from_recv(buf, (0, 1, 2), -1.0)):
            a = []
            for xl in range(4):
                cos, sin = small[32 + xl : 33 + xl], small[36 + xl : 37 + xl]
                b = re[16 * xl : 16 * xl + 16], im[16 * xl : 16 * xl + 16]
                a.append(b if xl == 0 else turn(*b, cos, sin, -1.0))
            for k, (zr, zi) in enumerate(quarter(a, -1.0)):
                spec[step, i, 0, :, 128 * k : 128 * k + 128] = zr
                spec[step, i, 1, :, 128 * k : 128 * k + 128] = zi

    def quarter(a, sign):
        (ar, ai), (br, bi), (cr, ci), (dr, di) = a
        pr, pi, mr, mi = ar + cr, ai + ci, ar - cr, ai - ci
        qr, qi, nr, ni = br + dr, bi + di, br - dr, bi - di
        tr, ti = -sign * ni, sign * nr
        return ((pr + qr, pi + qi), (mr + tr, mi + ti), (pr - qr, pi - qi), (mr - tr, mi - ti))

    def spectrum_inverse(loads_, out):
        blocks = []
        for re, im in loads_:
            a = [(re[:, 128 * k : 128 * k + 128], im[:, 128 * k : 128 * k + 128]) for k in range(4)]
            res, ims = [], []
            for xl, (zr, zi) in enumerate(quarter(a, 1.0)):
                if xl:
                    cos, sin = small[32 + xl : 33 + xl], small[36 + xl : 37 + xl]
                    zr, zi = turn(zr, zi, cos, sin, 1.0)
                res.append(zr)
                ims.append(zi)
            blocks.append((jnp.concatenate(res, axis=0), jnp.concatenate(ims, axis=0)))
        to_send(blocks, 1.0, out)

    def convolve_past(step):
        for i in range(3):
            def lag(m, acc):
                kr, ki = ker[m, i, 0].astype(F32), ker[m, i, 1].astype(F32)
                hr, hi = his[m - 1 - step, i, 0].astype(F32), his[m - 1 - step, i, 1].astype(F32)
                return acc[0] + (kr * hr - ki * hi), acc[1] + (kr * hi + ki * hr)

            zero = jnp.zeros((16, 512), F32)
            re, im = lax.fori_loop(1 + step, 12, lag, (zero, zero))
            part[step, i, 0], part[step, i, 1] = re, im

    def add_lag(i, m, step, re, im):
        kr, ki = ker[m, i, 0].astype(F32), ker[m, i, 1].astype(F32)
        sr, si = spec[step, i, 0], spec[step, i, 1]
        return re + (kr * sr - ki * si), im + (kr * si + ki * sr)

    def finish(copies):
        for copy in copies:
            copy.wait()

    finish(stress_loads)
    halo_top = make_halo(0, spad, stress_y, top)
    halo_deep = make_halo(1, spad, stress_y, deep)
    finish(conv_loads)
    convolve_past(0)
    pl.semaphore_wait(barrier, len(near))
    begin(halo_top)
    for mate in along_z:
        greet(ready_z, *mate)
    begin(halo_deep)
    convolve_past(1)
    finish(coef_loads)
    vel_load.wait()
    finish(halo_top)
    new_velocity(edges_of(0), top, 0)
    pl.semaphore_wait(ready_z, len(along_z))
    own = send_top(0)
    for mate in along_y:
        greet(ready_y, *mate)
    own_b = send_rows(4, lambda t: coef.at[0, 0, four(t), :], lambda t: buo_rows.at[four(t), :])
    finish(halo_deep)
    both = edges_of(1)
    for layer in deep:
        new_velocity(both, deep, layer)
    halo = start_halo(2, vpad, vel_y, deep4)
    finish(table_loads)
    wait_top(0, own)
    rows_forward([rows_in[0, i] for i in range(3)], send_a.at[0])
    pl.semaphore_wait(ready_y, len(along_y))
    own = send_all(0, send_a.at[0], recv_a.at[0])

    finish(coef_late)
    finish(halo)
    both = edges_of(2)
    new_stress(both, 0)
    halo_top = start_halo(3, spad, stress_y, top)
    for layer in deep:
        new_stress(both, layer)
    halo_deep = start_halo(4, spad, stress_y, deep)

    wait_all(0, own, recv_a.at[0])
    spectrum_forward(recv_a.at[0], 0)
    now = [add_lag(i, 0, 0, part[0, i, 0], part[0, i, 1]) for i in range(3)]
    ax = [small[40 + k : 41 + k] for k in range(4)]
    ay = along[...]

    def slope(xs, ys):
        return jnp.concatenate(
            [
                ax[k] * xs[:, 128 * k : 128 * k + 128] + ay * ys[:, 128 * k : 128 * k + 128]
                for k in range(4)
            ],
            axis=1,
        )

    slopes = (-slope(now[0][1], now[1][1]), slope(now[0][0], now[1][0]))
    spectrum_inverse([slopes], send_w)

    send_all(1, send_w, recv_w, order[:80])
    finish(halo_top)
    new_velocity(edges_of(3), top, 0)
    own_top = send_top(2)
    own = send_all(1, send_w, recv_w, order[80:])
    spectrum_inverse(now, send_b.at[0])
    own_t = send_all(4, send_b.at[0], recv_b.at[0])
    wait_rows(4, own_b, buo_rows.at[pl.ds(0, 60), :])
    wait_top(2, own_top)

    wait_all(1, own, recv_w)
    (slope_rows,) = rows_inverse(recv_w, (0,))
    rows_forward(
        [rows_in[1, 0], rows_in[1, 1], rows_in[1, 2] + buo_rows[...] * slope_rows], send_a.at[1]
    )
    own = send_all(2, send_a.at[1], recv_a.at[1])

    wait_all(4, own_t, recv_b.at[0])
    for i, t in enumerate(rows_inverse(recv_b.at[0], (0, 1, 2))):
        rows_out[0, i] = t
    rows_out[0, 3] = slope_rows
    own_trac = send_traction(1, 4)
    finish(halo_deep)
    both = edges_of(4)
    for layer in deep:
        new_velocity(both, deep, layer)
    for i in range(3):
        re, im = add_lag(i, 1, 0, part[1, i, 0], part[1, i, 1])
        part[1, i, 0], part[1, i, 1] = re, im

    wait_all(2, own, recv_a.at[1])
    spectrum_forward(recv_a.at[1], 1)
    spectrum_inverse(
        [add_lag(i, 0, 1, part[1, i, 0], part[1, i, 1]) for i in range(3)], send_b.at[1]
    )
    own = send_all(3, send_b.at[1], recv_b.at[1])

    wait_traction(1, own_trac, 4)
    inner = pl.ds(8, 64)
    for i in range(3):
        t = trac[0, i]
        vpad[i, 1, inner, :] = vpad[i, 1, inner, :] - NEAR * (coef[0, 1] * t)
        vpad[i, 2, inner, :] = vpad[i, 2, inner, :] - FAR * (coef[0, 2] * t)
        k = (XZ, YZ, ZZ)[i]
        spad[k, 0, inner, :] = spad[k, 0, inner, :] + t
    vpad[2, 0, inner, :] = vpad[2, 0, inner, :] + coef[0, 0] * trac[0, 3]
    halo = start_halo(5, vpad, vel_y, deep4)
    for i in range(3):
        for layer in range(4):
            vel_out[i, layer] = vpad[i, layer, inner, :]

    wait_all(3, own, recv_b.at[1])
    for i, t in enumerate(rows_inverse(recv_b.at[1], (0, 1, 2))):
        rows_out[1, i] = t
    own_trac = send_traction(3, 3)
    finish(halo)
    both = edges_of(5)
    for layer in range(4):
        new_stress(both, layer, str_out)
    wait_traction(3, own_trac, 3)
    for i, k in enumerate((XZ, YZ, ZZ)):
        str_out[PLACE[k], 0] = str_out[PLACE[k], 0] + trac[1, i]


def store_body(*refs):
    half = len(refs) // 2
    copies = [
        pltpu.make_async_copy(refs[i], refs[half + i], refs[-1].at[i]) for i in range(half)
    ]
    for copy in copies:
        copy.start()
    for copy in copies:
        copy.wait()


def on_device(velocity, stress, buoyancy, lame, shear, kernel, history):
    left, right, first, last, small, along = (jnp.asarray(t) for t in tables())
    anyspace = pl.BlockSpec(memory_space=pl.ANY)
    vm, dma = pltpu.VMEM, pltpu.SemaphoreType.DMA
    shapes = (
        jax.ShapeDtypeStruct(velocity.shape, F32),
        jax.ShapeDtypeStruct(stress.shape, F32),
        jax.ShapeDtypeStruct((2, 3, 2, 16, 512), F32),
    )
    results = pl.pallas_call(
        kernel_body,
        out_shape=tuple(vm(s.shape, s.dtype) for s in shapes),
        in_specs=[anyspace] * 13,
        out_specs=[pl.BlockSpec(memory_space=pltpu.VMEM)] * 3,
        scratch_shapes=[
            vm((3, 4, 80, 128), F32),
            vm((6, 4, 80, 128), F32),
            vm((3, 4, 64, 128), F32),
            vm((12, 3, 2, 16, 512), BF16),
            vm((11, 3, 2, 16, 512), BF16),
            vm((128, 768), BF16),
            vm((384, 256), BF16),
            vm((128, 256), BF16),
            vm((64, 384), BF16),
            vm((48, 128), F32),
            vm((16, 128), F32),
            vm((6, 64, 128), F32),
            vm((6, 64, 128), F32),
            vm((6, 64, 128), F32),
            vm((2, 3, 64, 128), F32),
            vm((64, 128), F32),
            vm((2, 128, 3, 128), F32),
            vm((2, 128, 3, 128), F32),
            vm((2, 128, 3, 128), F32),
            vm((2, 128, 3, 128), F32),
            vm((128, 1, 128), F32),
            vm((128, 1, 128), F32),
            vm((2, 4, 64, 128), F32),
            vm((2, 4, 64, 128), F32),
            vm((2, 3, 2, 16, 512), F32),
            dma((18,)),
            dma((6, 4)),
            dma((6, 4)),
            dma((5,)),
            dma((5,)),
            dma((5,)),
            dma((5,)),
            dma((10,)),
            pltpu.SemaphoreType.REGULAR,
            pltpu.SemaphoreType.REGULAR,
        ],
        compiler_params=pltpu.CompilerParams(
            collective_id=0, has_side_effects=True, vmem_limit_bytes=56 << 20
        ),
    )(
        velocity, stress, buoyancy, lame, shear, kernel, history,
        left, right, first, last, small, along,
    )
    return pl.pallas_call(
        store_body,
        out_shape=shapes,
        in_specs=[anyspace] * 3,
        out_specs=[anyspace] * 3,
        scratch_shapes=[dma((3,))],
        compiler_params=pltpu.CompilerParams(vmem_limit_bytes=1 << 20),
    )(*results)


def solution(mesh):
    spread = P(None, None, None, ("row", "col"), None)
    return jax.shard_map(
        on_device,
        mesh=mesh,
        in_specs=(
            P(None, None, "row", "col"),
            P(None, None, "row", "col"),
            P(None, "row", "col"),
            P(None, "row", "col"),
            P(None, "row", "col"),
            spread,
            spread,
        ),
        out_specs=(P(None, None, "row", "col"), P(None, None, "row", "col"), spread),
        check_vma=False,
    )
```

```python
import math

import jax
import jax.numpy as jnp
import numpy as np
from jax import lax
from jax.experimental import pallas as pl
from jax.experimental.pallas import tpu as pltpu
from jax.sharding import PartitionSpec as P

MESH = pl.DeviceIdType.MESH
F32, BF16 = jnp.float32, jnp.bfloat16
ROWS, COLS, DEVS = 8, 16, 128
NEAR, FAR = 2.0 / 3.0, -1.0 / 12.0
PLACE = (0, 3, 4, 1, 5, 2)
XX, XY, XZ, YY, YZ, ZZ = range(6)


def tables():
    def halves(a):
        hi = a.astype(BF16)
        lo = (a - hi.astype(np.float64)).astype(BF16)
        return hi, lo

    i128 = np.arange(128)
    ang = 2 * np.pi * (np.outer(i128, i128) % 128) / 128
    cos, sin = np.cos(ang), np.sin(ang)
    hi, lo = halves(np.concatenate([cos, sin], axis=1))
    left = np.concatenate([hi, hi, lo], axis=1)
    right = np.concatenate([hi, hi, lo], axis=0)
    j, c = np.arange(16), np.arange(16)
    ang = 2 * np.pi * (np.outer(j, c) % 16) / 16
    one = np.zeros((2, 4, 16, 16, 4))
    for xl in range(4):
        one[0, xl, :, :, xl] = np.cos(ang)
        one[1, xl, :, :, xl] = -np.sin(ang)
    one = one.reshape(128, 64) / 1024.0
    hi, lo = halves(one)
    first = np.concatenate([hi, hi, lo, lo], axis=1)
    hi, lo = halves(one.T)
    last = np.concatenate([hi, hi, lo], axis=1)
    small = np.zeros((48, 128), np.float32)
    ang = 2 * np.pi * np.outer(j, i128) / 2048
    small[0:16], small[16:32] = np.cos(ang), np.sin(ang)
    ang = 2 * np.pi * np.outer(np.arange(4), i128) / 512
    small[32:36], small[36:40] = np.cos(ang), np.sin(ang)
    th = 2 * np.pi * np.arange(512) / 512
    small[40:44] = (4 / 3 * np.sin(th) - 1 / 6 * np.sin(2 * th)).reshape(4, 128)
    th = 2 * np.pi * np.arange(2048) / 2048
    along = (4 / 3 * np.sin(th) - 1 / 6 * np.sin(2 * th)).reshape(128, 16, 1)
    along = np.broadcast_to(along, (128, 16, 128)).astype(np.float32)
    return left, right, first, last, small, along


def far_first(count):
    ring = (0, 1, 2, 1)

    def way(k):
        row, col = k // COLS, k % COLS
        z = 2 * (col // 8) + row % 2
        return ring[row // 2] + ring[z] + ring[col // 2 % 4] + 0.1 * (col % 2)

    return sorted(range(1, count), key=way, reverse=True)


def halves(x):
    hi = x.astype(BF16)
    return hi, (x - hi.astype(F32)).astype(BF16)


def dot(a, b, contract=((1,), (0,))):
    return lax.dot_general(a, b, (contract, ((), ())), preferred_element_type=F32)


def kernel_body(
    vel_in, str_in, buo_in, lam_in, she_in, ker_in, his_in,
    left_in, right_in, first_in, last_in, small_in, along_in,
    vel_out, str_out, spec,
    vpad, spad, coef, ker, his, left, right, first, last, small, along,
    pack, pack_low, pack_high, rows_in, buo_rows, send_a, recv_a, send_b, recv_b, send_w, recv_w,
    rows_out, trac, part,
    in_sem, halo_send, halo_recv, col_send, col_recv, all_send, all_recv, own_sem, ready_z, ready_y,
):
    r, c = lax.axis_index("row"), lax.axis_index("col")
    me = r * COLS + c

    def greet(semaphore, row, col):
        pl.semaphore_signal(semaphore, inc=1, device_id=(row, col), device_id_type=MESH)

    up, down = (lax.rem(r + 1, ROWS), c), (lax.rem(r + ROWS - 1, ROWS), c)
    after, before = (r, lax.rem(c + 1, COLS)), (r, lax.rem(c + COLS - 1, COLS))
    along_z = [(r, c ^ 8), (r ^ 1, c), (r ^ 1, c ^ 8)]
    along_y = [(r ^ 4, c), (r ^ 2, c), (r ^ 6, c)]
    along_x = [(r, c ^ k) for k in (5, 4, 7, 6, 3, 2, 1)]
    near = [after, before, up, down, *along_y, *along_z, *along_x]

    barrier = pltpu.get_barrier_semaphore()
    for mate in near:
        greet(barrier, *mate)
    loads = []

    def load(src, dst):
        copy = pltpu.make_async_copy(src, dst, in_sem.at[len(loads)])
        copy.start()
        loads.append(copy)
        return copy

    stress_loads = [
        load(str_in.at[PLACE[k]], spad.at[k, :, pl.ds(8, 64), :]) for k in range(6)
    ]
    coef_loads = [load(buo_in, coef.at[0])]
    vel_load = load(vel_in, vpad.at[:, :, pl.ds(8, 64), :])
    conv_loads = [load(ker_in, ker), load(his_in, his)]
    table_loads = [
        load(left_in, left), load(right_in, right), load(first_in, first),
        load(last_in, last), load(small_in, small), load(along_in.at[me], along),
    ]
    coef_late = [load(lam_in, coef.at[1]), load(she_in, coef.at[2])]

    lane = lax.broadcasted_iota(jnp.int32, (64, 128), 1)
    edge = jnp.logical_or(lane < 2, lane >= 126)

    def make_halo(n, pad, comps, layers):
        packed = jnp.zeros((64, 128), F32)
        for k in range(3 * len(layers)):
            comp, layer = comps[k // len(layers)], layers[k % len(layers)]
            f = pad[comp, layer, pl.ds(8, 64), :]
            packed += pltpu.roll(jnp.where(edge, f, 0.0), 4 * k + 2, 1)
        pack[n] = packed

        def remote(i, src, dst, to):
            copy = pltpu.make_async_remote_copy(
                src_ref=src, dst_ref=dst, send_sem=halo_send.at[n, i],
                recv_sem=halo_recv.at[n, i], device_id=to, device_id_type=MESH,
            )
            return copy

        some = pl.ds(layers[0], len(layers))
        copies = [
            remote(0, pad.at[pl.ds(0, 3), some, pl.ds(64, 8), :],
                   pad.at[pl.ds(0, 3), some, pl.ds(0, 8), :], up),
            remote(1, pad.at[pl.ds(0, 3), some, pl.ds(8, 8), :],
                   pad.at[pl.ds(0, 3), some, pl.ds(72, 8), :], down),
            remote(2, pack.at[n], pack_low.at[n], after),
            remote(3, pack.at[n], pack_high.at[n], before),
        ]
        return copies

    def begin(copies):
        for copy in copies:
            copy.start()

    def start_halo(n, pad, comps, layers):
        copies = make_halo(n, pad, comps, layers)
        begin(copies)
        return copies

    def edges_of(n):
        return jnp.where(lax.rem(lane, 4) >= 2, pack_high[n], pack_low[n])

    def dx(pad, comp, layer):
        def at(o):
            return pad[comp, layer, pl.ds(8 + o, 64), :]

        return NEAR * (at(1) - at(-1)) + FAR * (at(2) - at(-2))

    def dy(f, both, k):
        e = pltpu.roll(both, 128 - (4 * k + 2), 1)
        p1 = pltpu.roll(jnp.where(lane == 0, e, f), 127, 1)
        p2 = pltpu.roll(jnp.where(lane < 2, e, f), 126, 1)
        m1 = pltpu.roll(jnp.where(lane == 127, e, f), 1, 1)
        m2 = pltpu.roll(jnp.where(lane >= 126, e, f), 2, 1)
        return NEAR * (p1 - m1) + FAR * (p2 - m2)

    def dz(pad, comp, layer):
        total = None
        for o, w in ((1, NEAR), (-1, -NEAR), (2, FAR), (-2, -FAR)):
            if 0 <= layer + o < 4:
                term = w * pad[comp, layer + o, pl.ds(8, 64), :]
                total = term if total is None else total + term
        return total

    stress_y, vel_y = (XY, YY, YZ), (0, 1, 2)
    top, deep, deep4 = (0,), (1, 2, 3), (0, 1, 2, 3)

    def new_velocity(both, layers, layer):
        along_x = [dx(spad, k, layer) for k in (XX, XY, XZ)]
        along_y = [
            dy(spad[k, layer, pl.ds(8, 64), :], both, len(layers) * i + layer - layers[0])
            for i, k in enumerate((XY, YY, YZ))
        ]
        along_z = [dz(spad, k, layer) for k in (XZ, YZ, ZZ)]
        b = coef[0, layer]
        for i in range(3):
            vpad[i, layer, pl.ds(8, 64), :] = vpad[i, layer, pl.ds(8, 64), :] + b * (
                along_x[i] + along_y[i] + along_z[i]
            )

    def new_stress(both, layer, out=None):
        gx = [dx(vpad, i, layer) for i in range(3)]
        gy = [dy(vpad[i, layer, pl.ds(8, 64), :], both, 4 * i + layer) for i in range(3)]
        gz = [dz(vpad, i, layer) for i in range(3)]
        lam, she = coef[1, layer], coef[2, layer]
        spread = lam * (gx[0] + gy[1] + gz[2])
        adds = {
            XX: spread + 2.0 * she * gx[0], YY: spread + 2.0 * she * gy[1],
            ZZ: spread + 2.0 * she * gz[2], XY: she * (gy[0] + gx[1]),
            XZ: she * (gz[0] + gx[2]), YZ: she * (gz[1] + gy[2]),
        }
        for k, a in adds.items():
            total = spad[k, layer, pl.ds(8, 64), :] + a
            if out is None:
                spad[k, layer, pl.ds(8, 64), :] = total
            else:
                out[PLACE[k], layer] = total

    def send_rows(n, src, dst):
        for k in far_first(COLS):
            t = c ^ k
            pltpu.make_async_remote_copy(
                src_ref=src(t), dst_ref=dst(c), send_sem=col_send.at[n],
                recv_sem=col_recv.at[n], device_id=(r, t), device_id_type=MESH,
            ).start()
        own = pltpu.make_async_copy(src(c), dst(c), own_sem.at[n])
        own.start()
        return own

    def wait_rows(n, own, whole):
        copy = pltpu.make_async_remote_copy(
            src_ref=whole, dst_ref=whole, send_sem=col_send.at[n],
            recv_sem=col_recv.at[n], device_id=after, device_id_type=MESH,
        )
        copy.wait()
        own.wait()

    def four(t):
        return pl.ds(pl.multiple_of(4 * t, 4), 4)

    def send_top(n):
        return send_rows(
            n, lambda t: vpad.at[:, 0, pl.ds(pl.multiple_of(8 + 4 * t, 4), 4), :],
            lambda t: rows_in.at[n // 2, :, four(t), :],
        )

    def wait_top(n, own):
        wait_rows(n, own, rows_in.at[n // 2, :, pl.ds(0, 60), :])

    def send_traction(n, count):
        return send_rows(
            n, lambda t: rows_out.at[n // 2, pl.ds(0, count), four(t), :],
            lambda t: trac.at[n // 2, pl.ds(0, count), four(t), :],
        )

    def wait_traction(n, own, count):
        wait_rows(n, own, trac.at[n // 2, pl.ds(0, count), pl.ds(0, 60), :])

    order = far_first(DEVS)

    def send_all(n, src, dst, some=order):
        for k in some:
            pltpu.make_async_remote_copy(
                src_ref=src.at[me ^ k], dst_ref=dst.at[me], send_sem=all_send.at[n],
                recv_sem=all_recv.at[n], device_id=(r ^ (k // COLS), c ^ (k % COLS)),
                device_id_type=MESH,
            ).start()
        if some[-1] != order[-1]:
            return None
        own = pltpu.make_async_copy(src.at[me], dst.at[me], own_sem.at[5 + n])
        own.start()
        return own

    def wait_all(n, own, dst):
        whole = dst.at[pl.ds(0, DEVS - 1)]
        copy = pltpu.make_async_remote_copy(
            src_ref=whole, dst_ref=whole, send_sem=all_send.at[n],
            recv_sem=all_recv.at[n], device_id=after, device_id_type=MESH,
        )
        copy.wait()
        own.wait()

    def turn(re, im, cos, sin, sign):
        return re * cos - im * (sign * sin), im * cos + re * (sign * sin)

    def to_send(blocks, sign, out, place=0):
        data = []
        for re, im in blocks:
            data.append(jnp.concatenate([re, -sign * im], axis=1))
            data.append(jnp.concatenate([im, sign * re], axis=1))
        hi, lo = halves(jnp.concatenate(data, axis=0))
        full = dot(left[...], jnp.concatenate([hi, lo, hi], axis=1), ((1,), (1,)))
        for i in range(len(blocks)):
            out[:, place + i, :] = full[:, 128 * i : 128 * i + 128]

    def from_recv(buf, which, sign):
        turned = [buf[:, i, :].T for i in which]
        hi, lo = halves(jnp.concatenate(turned, axis=0))
        full = dot(jnp.concatenate([hi, lo, hi], axis=1), right[...])
        result = []
        for i in range(len(turned)):
            a = full[128 * i : 128 * i + 128]
            p, q = a[:, :128], a[:, 128:]
            result.append((p[:64] - sign * q[64:], p[64:] + sign * q[:64]))
        return result

    def rows_forward(fields, out, place=0):
        hi, lo = halves(jnp.concatenate(fields, axis=1))
        mixed = dot(first[...], jnp.concatenate([hi, lo, hi, lo], axis=0))
        cos, sin = small[0:16][None], small[16:32][None]
        blocks = []
        for i in range(len(fields)):
            a = mixed[:, 128 * i : 128 * i + 128]
            re, im = a[:64].reshape(4, 16, 128), a[64:].reshape(4, 16, 128)
            re, im = turn(re, im, cos, sin, -1.0)
            blocks.append((re.reshape(64, 128), im.reshape(64, 128)))
        to_send(blocks, -1.0, out, place)

    def rows_inverse(buf, which):
        cos, sin = small[0:16][None], small[16:32][None]
        parts = []
        for re, im in from_recv(buf, which, 1.0):
            re, im = turn(re.reshape(4, 16, 128), im.reshape(4, 16, 128), cos, sin, 1.0)
            parts.append(
                jnp.concatenate([re.reshape(64, 128), im.reshape(64, 128)], axis=0)
            )
        hi, lo = halves(jnp.concatenate(parts, axis=1))
        full = dot(last[...], jnp.concatenate([hi, lo, hi], axis=0))
        return [full[:, 128 * i : 128 * i + 128] for i in range(len(parts))]

    def spectrum_forward(buf, step):
        for i, (re, im) in enumerate(from_recv(buf, (0, 1, 2), -1.0)):
            a = []
            for xl in range(4):
                cos, sin = small[32 + xl : 33 + xl], small[36 + xl : 37 + xl]
                b = re[16 * xl : 16 * xl + 16], im[16 * xl : 16 * xl + 16]
                a.append(b if xl == 0 else turn(*b, cos, sin, -1.0))
            for k, (zr, zi) in enumerate(quarter(a, -1.0)):
                spec[step, i, 0, :, 128 * k : 128 * k + 128] = zr
                spec[step, i, 1, :, 128 * k : 128 * k + 128] = zi

    def quarter(a, sign):
        (ar, ai), (br, bi), (cr, ci), (dr, di) = a
        pr, pi, mr, mi = ar + cr, ai + ci, ar - cr, ai - ci
        qr, qi, nr, ni = br + dr, bi + di, br - dr, bi - di
        tr, ti = -sign * ni, sign * nr
        return ((pr + qr, pi + qi), (mr + tr, mi + ti), (pr - qr, pi - qi), (mr - tr, mi - ti))

    def spectrum_inverse(loads_, out):
        blocks = []
        for re, im in loads_:
            a = [(re[:, 128 * k : 128 * k + 128], im[:, 128 * k : 128 * k + 128]) for k in range(4)]
            res, ims = [], []
            for xl, (zr, zi) in enumerate(quarter(a, 1.0)):
                if xl:
                    cos, sin = small[32 + xl : 33 + xl], small[36 + xl : 37 + xl]
                    zr, zi = turn(zr, zi, cos, sin, 1.0)
                res.append(zr)
                ims.append(zi)
            blocks.append((jnp.concatenate(res, axis=0), jnp.concatenate(ims, axis=0)))
        to_send(blocks, 1.0, out)

    def convolve_past(step):
        for i in range(3):
            def lag(m, acc):
                kr, ki = ker[m, i, 0].astype(F32), ker[m, i, 1].astype(F32)
                hr, hi = his[m - 1 - step, i, 0].astype(F32), his[m - 1 - step, i, 1].astype(F32)
                return acc[0] + (kr * hr - ki * hi), acc[1] + (kr * hi + ki * hr)

            zero = jnp.zeros((16, 512), F32)
            re, im = lax.fori_loop(1 + step, 12, lag, (zero, zero))
            part[step, i, 0], part[step, i, 1] = re, im

    def add_lag(i, m, step, re, im):
        kr, ki = ker[m, i, 0].astype(F32), ker[m, i, 1].astype(F32)
        sr, si = spec[step, i, 0], spec[step, i, 1]
        return re + (kr * sr - ki * si), im + (kr * si + ki * sr)

    def finish(copies):
        for copy in copies:
            copy.wait()

    finish(stress_loads)
    halo_top = make_halo(0, spad, stress_y, top)
    halo_deep = make_halo(1, spad, stress_y, deep)
    finish(conv_loads)
    convolve_past(0)
    pl.semaphore_wait(barrier, len(near))
    begin(halo_top)
    for mate in along_z:
        greet(ready_z, *mate)
    begin(halo_deep)
    convolve_past(1)
    finish(coef_loads)
    vel_load.wait()
    finish(halo_top)
    new_velocity(edges_of(0), top, 0)
    pl.semaphore_wait(ready_z, len(along_z))
    own = send_top(0)
    for mate in along_y:
        greet(ready_y, *mate)
    finish(halo_deep)
    both = edges_of(1)
    for layer in deep:
        new_velocity(both, deep, layer)
    halo = start_halo(2, vpad, vel_y, deep4)
    finish(table_loads)
    wait_top(0, own)
    rows_forward([rows_in[0, i] for i in range(3)], send_a.at[0])
    pl.semaphore_wait(ready_y, len(along_y))
    own = send_all(0, send_a.at[0], recv_a.at[0])
    own_b = send_rows(4, lambda t: coef.at[0, 0, four(t), :], lambda t: buo_rows.at[four(t), :])

    finish(coef_late)
    finish(halo)
    both = edges_of(2)
    new_stress(both, 0)
    halo_top = start_halo(3, spad, stress_y, top)
    for layer in deep:
        new_stress(both, layer)
    halo_deep = start_halo(4, spad, stress_y, deep)

    wait_all(0, own, recv_a.at[0])
    spectrum_forward(recv_a.at[0], 0)
    now = [add_lag(i, 0, 0, part[0, i, 0], part[0, i, 1]) for i in range(3)]
    ax = [small[40 + k : 41 + k] for k in range(4)]
    ay = along[...]

    def slope(xs, ys):
        return jnp.concatenate(
            [
                ax[k] * xs[:, 128 * k : 128 * k + 128] + ay * ys[:, 128 * k : 128 * k + 128]
                for k in range(4)
            ],
            axis=1,
        )

    slopes = (-slope(now[0][1], now[1][1]), slope(now[0][0], now[1][0]))
    spectrum_inverse([slopes], send_w)

    send_all(1, send_w, recv_w, order[:80])
    finish(halo_top)
    new_velocity(edges_of(3), top, 0)
    own_top = send_top(2)
    own = send_all(1, send_w, recv_w, order[80:])
    spectrum_inverse(now, send_b.at[0])
    own_t = send_all(4, send_b.at[0], recv_b.at[0])
    wait_rows(4, own_b, buo_rows.at[pl.ds(0, 60), :])
    wait_top(2, own_top)
    rows_forward([rows_in[1, 0], rows_in[1, 1]], send_a.at[1])

    wait_all(1, own, recv_w)
    (slope_rows,) = rows_inverse(recv_w, (0,))
    rows_forward([rows_in[1, 2] + buo_rows[...] * slope_rows], send_a.at[1], 2)
    own = send_all(2, send_a.at[1], recv_a.at[1])

    wait_all(4, own_t, recv_b.at[0])
    for i, t in enumerate(rows_inverse(recv_b.at[0], (0, 1, 2))):
        rows_out[0, i] = t
    rows_out[0, 3] = slope_rows
    own_trac = send_traction(1, 4)
    finish(halo_deep)
    both = edges_of(4)
    for layer in deep:
        new_velocity(both, deep, layer)
    for i in range(3):
        re, im = add_lag(i, 1, 0, part[1, i, 0], part[1, i, 1])
        part[1, i, 0], part[1, i, 1] = re, im

    wait_all(2, own, recv_a.at[1])
    spectrum_forward(recv_a.at[1], 1)
    spectrum_inverse(
        [add_lag(i, 0, 1, part[1, i, 0], part[1, i, 1]) for i in range(3)], send_b.at[1]
    )
    own = send_all(3, send_b.at[1], recv_b.at[1])

    wait_traction(1, own_trac, 4)
    inner = pl.ds(8, 64)
    for i in range(3):
        t = trac[0, i]
        vpad[i, 1, inner, :] = vpad[i, 1, inner, :] - NEAR * (coef[0, 1] * t)
        vpad[i, 2, inner, :] = vpad[i, 2, inner, :] - FAR * (coef[0, 2] * t)
        k = (XZ, YZ, ZZ)[i]
        spad[k, 0, inner, :] = spad[k, 0, inner, :] + t
    vpad[2, 0, inner, :] = vpad[2, 0, inner, :] + coef[0, 0] * trac[0, 3]
    halo = start_halo(5, vpad, vel_y, deep4)
    for i in range(3):
        for layer in range(4):
            vel_out[i, layer] = vpad[i, layer, inner, :]

    wait_all(3, own, recv_b.at[1])
    for i, t in enumerate(rows_inverse(recv_b.at[1], (0, 1, 2))):
        rows_out[1, i] = t
    own_trac = send_traction(3, 3)
    finish(halo)
    both = edges_of(5)
    for layer in range(4):
        new_stress(both, layer, str_out)
    wait_traction(3, own_trac, 3)
    for i, k in enumerate((XZ, YZ, ZZ)):
        str_out[PLACE[k], 0] = str_out[PLACE[k], 0] + trac[1, i]


def store_body(*refs):
    half = len(refs) // 2
    copies = [
        pltpu.make_async_copy(refs[i], refs[half + i], refs[-1].at[i]) for i in range(half)
    ]
    for copy in copies:
        copy.start()
    for copy in copies:
        copy.wait()


def on_device(velocity, stress, buoyancy, lame, shear, kernel, history):
    left, right, first, last, small, along = (jnp.asarray(t) for t in tables())
    anyspace = pl.BlockSpec(memory_space=pl.ANY)
    vm, dma = pltpu.VMEM, pltpu.SemaphoreType.DMA
    shapes = (
        jax.ShapeDtypeStruct(velocity.shape, F32),
        jax.ShapeDtypeStruct(stress.shape, F32),
        jax.ShapeDtypeStruct((2, 3, 2, 16, 512), F32),
    )
    results = pl.pallas_call(
        kernel_body,
        out_shape=tuple(vm(s.shape, s.dtype) for s in shapes),
        in_specs=[anyspace] * 13,
        out_specs=[pl.BlockSpec(memory_space=pltpu.VMEM)] * 3,
        scratch_shapes=[
            vm((3, 4, 80, 128), F32),
            vm((6, 4, 80, 128), F32),
            vm((3, 4, 64, 128), F32),
            vm((12, 3, 2, 16, 512), BF16),
            vm((11, 3, 2, 16, 512), BF16),
            vm((128, 768), BF16),
            vm((384, 256), BF16),
            vm((128, 256), BF16),
            vm((64, 384), BF16),
            vm((48, 128), F32),
            vm((16, 128), F32),
            vm((6, 64, 128), F32),
            vm((6, 64, 128), F32),
            vm((6, 64, 128), F32),
            vm((2, 3, 64, 128), F32),
            vm((64, 128), F32),
            vm((2, 128, 3, 128), F32),
            vm((2, 128, 3, 128), F32),
            vm((2, 128, 3, 128), F32),
            vm((2, 128, 3, 128), F32),
            vm((128, 1, 128), F32),
            vm((128, 1, 128), F32),
            vm((2, 4, 64, 128), F32),
            vm((2, 4, 64, 128), F32),
            vm((2, 3, 2, 16, 512), F32),
            dma((18,)),
            dma((6, 4)),
            dma((6, 4)),
            dma((5,)),
            dma((5,)),
            dma((5,)),
            dma((5,)),
            dma((10,)),
            pltpu.SemaphoreType.REGULAR,
            pltpu.SemaphoreType.REGULAR,
        ],
        compiler_params=pltpu.CompilerParams(
            collective_id=0, has_side_effects=True, vmem_limit_bytes=56 << 20
        ),
    )(
        velocity, stress, buoyancy, lame, shear, kernel, history,
        left, right, first, last, small, along,
    )
    return pl.pallas_call(
        store_body,
        out_shape=shapes,
        in_specs=[anyspace] * 3,
        out_specs=[anyspace] * 3,
        scratch_shapes=[dma((3,))],
        compiler_params=pltpu.CompilerParams(vmem_limit_bytes=1 << 20),
    )(*results)


def solution(mesh):
    spread = P(None, None, None, ("row", "col"), None)
    return jax.shard_map(
        on_device,
        mesh=mesh,
        in_specs=(
            P(None, None, "row", "col"),
            P(None, None, "row", "col"),
            P(None, "row", "col"),
            P(None, "row", "col"),
            P(None, "row", "col"),
            spread,
            spread,
        ),
        out_specs=(P(None, None, "row", "col"), P(None, None, "row", "col"), spread),
        check_vma=False,
    )
```
